512 devices in a mesh: node: 32 (over x, z), feat: 16 (over y, core).
Axes of the slice: x: 4, y: 8, z: 8, core: 2. Of those that a mesh axis runs over, the one named last changes fastest.
Arguments:
- features: bfloat16 [16384, 4096], P('node', 'feat'), may hold values from -6 to 6
- own_features: bfloat16 [6144, 4096], P('node', 'feat'), may hold values from -6 to 6
- neigh_index: int32 [32, 6144, 4], P('node'), may hold values from 0 to 511
- neigh_count: int32 [32, 6144], P('node'), may hold values from 0 to 4, as said below
- degree: int32 [6144], P('node'), may hold values from 1 to 128, as said below
- local_index: int32 [6144, 10], P('node'), may hold values from 0 to 191
- local_count: int32 [6144], P('node'), may hold values from 0 to 10
- self_weight: bfloat16 [4096, 1024], P('feat'), may hold values from -0.09375 to 0.09375
- neigh_weight: bfloat16 [4096, 1024], P('feat'), may hold values from -0.09375 to 0.09375
- weight_two: bfloat16 [1024, 1024], replicated, may hold values from -0.1875 to 0.1875
- weight_three: bfloat16 [1024, 172], replicated, may hold values from -0.1875 to 0.1875
- cotangent: bfloat16 [6144, 172], P('node'), may hold values from -6 to 6
Outputs:
- grad_self: bfloat16 [4096, 1024], P('feat')
- grad_neigh: bfloat16 [4096, 1024], P('feat')
- logits: bfloat16 [6144, 172], P('node')
The draws below stay inside these ranges and needn't reach their ends.
Inputs may be any that keep to these rules, and one draw needn't show every extreme that they name: `neigh_count`: slab s is full (4 live slots) at row s. degree[r] is the sum of neigh_count[s, r] over all slabs s.
All inputs are finite; a program needn't handle non-finite values.
Results may differ from the reference program's by a relative error of at most 0.015.
Values may be sent and summed in bfloat16 or wider, within the bound.
No kernel may reach another device: no remote copies, remote signals or barrier semaphores. Data moves between devices by JAX's collectives and lax.ppermute only.
A program may use at most 64 MiB of HBM per device.

```python
import jax
import jax.numpy as jnp
from jax import lax

D = 4096
H = 1024
C = 172
FS = 4
F2 = 10
ROWS_DEV = 192
NODE_DEV = 512
TOTAL = 6144
NODES = 16384
N_NODE = 32


def slab_counts(key):
    key_hi, key_base, key_home = jax.random.split(key, 3)
    upper = jax.random.randint(key_hi, (N_NODE, 1), 1, FS + 1)
    base = jax.random.randint(key_base, (N_NODE, TOTAL), 0, FS + 1)
    counts = jnp.minimum(base, upper)
    home = jax.random.randint(key_home, (TOTAL,), 0, N_NODE)
    slab_ids = jnp.arange(N_NODE, dtype=jnp.int32)[:, None]
    row_ids = jnp.arange(TOTAL, dtype=jnp.int32)[None, :]
    counts = jnp.where(slab_ids == home[None, :], jnp.maximum(counts, 1), counts)
    counts = jnp.where(row_ids == TOTAL - 2, jnp.where(slab_ids == home[None, :], 1, 0), counts)
    counts = jnp.where(row_ids == TOTAL - 1, FS, counts)
    counts = jnp.where(row_ids == slab_ids, FS, counts)
    return counts.astype(jnp.int32)


def draw_neigh_count(key, part):
    return slab_counts(key)


def draw_degree(key, part):
    return jnp.sum(slab_counts(key), axis=0).astype(jnp.int32)


def plant(drawn, key, least, top_value):
    shape = drawn.shape
    place = [jax.random.randint(jax.random.fold_in(key, axis), (), 0, shape[axis]) for axis in range(len(shape))]
    drawn = drawn.at[tuple(place)].set(least)
    longest = shape.index(max(shape))
    place[longest] = (place[longest] + 1) % shape[longest]
    return drawn.at[tuple(place)].set(top_value)


def block_scale(key, dims, shards, least, top_value):
    level = 1.0
    for position, shards_of in shards:
        steps = jax.random.uniform(jax.random.fold_in(jax.random.fold_in(key, 6), position), (shards_of,), jnp.float32, least / len(shards), top_value / len(shards))
        level = level * jnp.repeat(jnp.exp(steps), dims[position] // shards_of).reshape((-1,) + (1,) * (len(dims) - 1 - position))
    return level


def centred(stream_key, extent, spread, limit, pieces=(), kind=jnp.bfloat16):
    result = jax.random.normal(stream_key, extent, jnp.float32) * spread
    if len(pieces) > 0:
        result = block_scale(stream_key, extent, pieces, -0.22, 0.18) * result
    return jnp.clip(result, min=-limit, max=limit).astype(kind)


def setup_inputs(seed: int = 0) -> dict:
    key_of = jax.random.split(jax.random.key(seed), 13)
    features = centred(key_of[0], (NODES, D), 1.0, 6.0, ((0, 32), (1, 16)))
    own_features = centred(key_of[1], (TOTAL, D), 1.0, 6.0, ((0, 32), (1, 16)))
    neigh_index = plant(jax.random.randint(key_of[2], (N_NODE, TOTAL, FS), 0, NODE_DEV), jax.random.fold_in(key_of[2], 1), 0, NODE_DEV - 1).astype(jnp.int32)
    neigh_count = draw_neigh_count(jax.random.fold_in(key_of[12], 71), 0)
    degree = draw_degree(jax.random.fold_in(key_of[12], 71), 0)
    local_index = plant(jax.random.randint(key_of[5], (TOTAL, F2), 0, ROWS_DEV), jax.random.fold_in(key_of[5], 1), 0, ROWS_DEV - 1).astype(jnp.int32)
    local_count = plant(jax.random.randint(key_of[6], (TOTAL,), 0, F2 + 1), jax.random.fold_in(key_of[6], 1), 0, F2).astype(jnp.int32)
    self_weight = centred(key_of[7], (D, H), D ** -0.5, 0.09375, ((0, 16),))
    neigh_weight = centred(key_of[8], (D, H), D ** -0.5, 0.09375, ((0, 16),))
    weight_two = centred(key_of[9], (H, H), H ** -0.5, 0.1875)
    weight_three = centred(key_of[10], (H, C), H ** -0.5, 0.1875)
    cotangent = centred(key_of[11], (TOTAL, C), 1.0, 6.0, ((0, 32),))
    return dict(features=features, own_features=own_features, neigh_index=neigh_index, neigh_count=neigh_count, degree=degree, local_index=local_index, local_count=local_count, self_weight=self_weight, neigh_weight=neigh_weight, weight_two=weight_two, weight_three=weight_three, cotangent=cotangent)


def silu_slope(value):
    gate = jax.nn.sigmoid(value)
    return gate + value * gate * (1.0 - gate)


def slab_partial(table, index, count):
    running = jnp.zeros((index.shape[0], table.shape[1]), jnp.float32)
    for slot in range(index.shape[1]):
        picked = table[index[:, slot]].astype(jnp.float32)
        running = running + jnp.where((count > slot)[:, None], picked, 0.0)
    return running.astype(jnp.bfloat16)


def second_layer(first_hidden, local_index, local_count, weight_two, weight_three, cotangent):
    row_count = first_hidden.shape[0]
    slot_ids = jnp.arange(local_index.shape[1], dtype=jnp.int32)
    live_slots = slot_ids[None, :] < local_count[:, None]
    slot_hits = (local_index[:, :, None] == jnp.arange(row_count, dtype=jnp.int32)[None, None, :]) & live_slots[:, :, None]
    adjacency = jnp.sum(slot_hits.astype(jnp.float32), axis=1) + jnp.eye(row_count, dtype=jnp.float32)
    inv_count = 1.0 / (1.0 + local_count.astype(jnp.float32))
    mixed_rows = (jnp.dot(adjacency.astype(jnp.bfloat16), first_hidden, preferred_element_type=jnp.float32) * inv_count[:, None]).astype(jnp.bfloat16)
    pre_two = jnp.dot(mixed_rows, weight_two, preferred_element_type=jnp.float32)
    second_hidden = jax.nn.silu(pre_two).astype(jnp.bfloat16)
    logits = jnp.dot(second_hidden, weight_three, preferred_element_type=jnp.float32).astype(jnp.bfloat16)
    back_two = jnp.dot(cotangent, weight_three.T, preferred_element_type=jnp.float32)
    grad_pre_two = (back_two * silu_slope(pre_two)).astype(jnp.bfloat16)
    grad_mixed = jnp.dot(grad_pre_two, weight_two.T, preferred_element_type=jnp.float32) * inv_count[:, None]
    grad_hidden = jnp.dot(adjacency.T, grad_mixed, precision=lax.Precision.HIGHEST, preferred_element_type=jnp.float32)
    return logits, grad_hidden


def reference(features, own_features, neigh_index, neigh_count, degree, local_index, local_count, self_weight, neigh_weight, weight_two, weight_three, cotangent):
    def add_slab(carry, slab):
        table = lax.dynamic_slice_in_dim(features, slab * NODE_DEV, NODE_DEV, 0)
        part = slab_partial(table, neigh_index[slab], neigh_count[slab])
        return carry + part.astype(jnp.float32), None

    start = jnp.zeros((TOTAL, D), jnp.float32)
    neighbour_sum, _ = lax.scan(add_slab, start, jnp.arange(N_NODE, dtype=jnp.int32))
    mean_rows = (neighbour_sum / degree[:, None].astype(jnp.float32)).astype(jnp.bfloat16)
    pre_one = jnp.dot(own_features, self_weight, preferred_element_type=jnp.float32) + jnp.dot(mean_rows, neigh_weight, preferred_element_type=jnp.float32)
    first_hidden = jax.nn.silu(pre_one).astype(jnp.bfloat16)
    slope_one = silu_slope(pre_one).astype(jnp.bfloat16)

    def one_owner(group):
        return second_layer(group[0], group[1], group[2], weight_two, weight_three, group[3])

    logits, grad_hidden = lax.map(one_owner, (first_hidden.reshape(N_NODE, ROWS_DEV, H), local_index.reshape(N_NODE, ROWS_DEV, F2), local_count.reshape(N_NODE, ROWS_DEV), cotangent.reshape(N_NODE, ROWS_DEV, C)))
    logits = logits.reshape(TOTAL, C)
    grad_hidden = grad_hidden.reshape(TOTAL, H)
    grad_pre_one = (grad_hidden * slope_one.astype(jnp.float32)).astype(jnp.bfloat16)
    grad_self = jnp.dot(own_features.T, grad_pre_one, preferred_element_type=jnp.float32).astype(jnp.bfloat16)
    grad_neigh = jnp.dot(mean_rows.T, grad_pre_one, preferred_element_type=jnp.float32).astype(jnp.bfloat16)
    return (grad_self, grad_neigh, logits)
```

```python
import math

import jax
import jax.numpy as jnp
from jax import lax
from jax.experimental import pallas as pl
from jax.experimental.pallas import tpu as pltpu
from jax.sharding import PartitionSpec as P


def silu_slope(value):
    gate = jax.nn.sigmoid(value)
    return gate + value * gate * (1.0 - gate)


def gather_kernel(index_ref, count_ref, table_ref, out_ref):
    slots, rows = index_ref.shape
    nodes = table_ref.shape[0]
    index = index_ref[...]
    count = count_ref[...]
    slot = lax.broadcasted_iota(jnp.int32, (slots, rows), 0)
    live = jnp.where(slot < count, index, -1)
    columns = jnp.concatenate([live, jnp.zeros((8 - slots, rows), jnp.int32)], axis=0).T
    node = lax.broadcasted_iota(jnp.int32, (rows, nodes), 1)
    hits = jnp.zeros((rows, nodes), jnp.float32)
    for k in range(slots):
        hits = hits + jnp.where(columns[:, k : k + 1] == node, 1.0, 0.0)
    out_ref[...] = jnp.dot(
        hits.astype(jnp.bfloat16), table_ref[...], preferred_element_type=jnp.float32
    ).astype(jnp.bfloat16)


def slab_partial(table, index, count):
    slots, total = index.shape
    block = math.gcd(total, 512)
    nodes, width = table.shape
    return pl.pallas_call(
        gather_kernel,
        grid=(total // block,),
        in_specs=[
            pl.BlockSpec((slots, block), lambda i: (0, i)),
            pl.BlockSpec((1, block), lambda i: (0, i)),
            pl.BlockSpec((nodes, width), lambda i: (0, 0)),
        ],
        out_specs=pl.BlockSpec((block, width), lambda i: (i, 0)),
        out_shape=jax.ShapeDtypeStruct((total, width), jnp.bfloat16),
        compiler_params=pltpu.CompilerParams(vmem_limit_bytes=32 * 1024 * 1024),
        name="slab_partial",
    )(index, count, table)


def second_layer(first_hidden, local_index, local_count, weight_two, weight_three, cotangent):
    row_count = first_hidden.shape[0]
    slot_ids = jnp.arange(local_index.shape[1], dtype=jnp.int32)
    live_slots = slot_ids[None, :] < local_count[:, None]
    slot_hits = (
        local_index[:, :, None] == jnp.arange(row_count, dtype=jnp.int32)[None, None, :]
    ) & live_slots[:, :, None]
    adjacency = jnp.sum(slot_hits.astype(jnp.float32), axis=1) + jnp.eye(
        row_count, dtype=jnp.float32
    )
    inv_count = 1.0 / (1.0 + local_count.astype(jnp.float32))
    mixed_rows = (
        jnp.dot(adjacency.astype(jnp.bfloat16), first_hidden, preferred_element_type=jnp.float32)
        * inv_count[:, None]
    ).astype(jnp.bfloat16)
    pre_two = jnp.dot(mixed_rows, weight_two, preferred_element_type=jnp.float32)
    second_hidden = jax.nn.silu(pre_two).astype(jnp.bfloat16)
    logits = jnp.dot(second_hidden, weight_three, preferred_element_type=jnp.float32).astype(
        jnp.bfloat16
    )
    back_two = jnp.dot(cotangent, weight_three.T, preferred_element_type=jnp.float32)
    grad_pre_two = (back_two * silu_slope(pre_two)).astype(jnp.bfloat16)
    grad_mixed = (
        jnp.dot(grad_pre_two, weight_two.T, preferred_element_type=jnp.float32) * inv_count[:, None]
    )
    grad_hidden = jnp.dot(
        adjacency.T, grad_mixed, precision=lax.Precision.HIGHEST, preferred_element_type=jnp.float32
    )
    return (logits, grad_hidden)


def exchange(pieces, axis):
    return lax.all_to_all(pieces, axis, split_axis=0, concat_axis=0, tiled=True)


def body(
    features,
    own_features,
    neigh_index,
    neigh_count,
    degree,
    local_index,
    local_count,
    self_weight,
    neigh_weight,
    weight_two,
    weight_three,
    cotangent,
):
    groups = lax.axis_size("node")
    splits = lax.axis_size("feat")
    parts = slab_partial(features, neigh_index[0].T, neigh_count)
    own_rows = parts.shape[0] // groups
    width = features.shape[1]
    neighbour_sum = jnp.sum(
        exchange(parts.reshape(groups, own_rows, width), "node").astype(jnp.float32), axis=0
    )
    mean_rows = (neighbour_sum / degree[:, None].astype(jnp.float32)).astype(jnp.bfloat16)
    pre_part = jnp.dot(own_features, self_weight, preferred_element_type=jnp.float32) + jnp.dot(
        mean_rows, neigh_weight, preferred_element_type=jnp.float32
    )
    hidden = pre_part.shape[1]
    halves = 2
    tiles = splits // halves
    pieces = (
        pre_part.astype(jnp.bfloat16)
        .reshape(halves, own_rows // halves, tiles, hidden // tiles)
        .transpose(2, 0, 1, 3)
        .reshape(splits, own_rows // halves, hidden // tiles)
    )
    pre_piece = jnp.sum(exchange(pieces, "feat").astype(jnp.float32), axis=0).astype(jnp.bfloat16)
    pre_one = (
        lax.all_gather(pre_piece, "feat", axis=0, tiled=False)
        .reshape(tiles, halves, own_rows // halves, hidden // tiles)
        .transpose(1, 2, 0, 3)
        .reshape(own_rows, hidden)
        .astype(jnp.float32)
    )
    first_hidden = jax.nn.silu(pre_one).astype(jnp.bfloat16)
    slope_one = silu_slope(pre_one).astype(jnp.bfloat16)
    logits, grad_hidden = second_layer(
        first_hidden, local_index, local_count, weight_two, weight_three, cotangent
    )
    grad_pre_one = (grad_hidden * slope_one.astype(jnp.float32)).astype(jnp.bfloat16)
    both = jnp.concatenate([own_features, mean_rows], axis=1)
    grad_part = jnp.dot(both.T, grad_pre_one, preferred_element_type=jnp.float32).astype(
        jnp.bfloat16
    )
    grad_piece = jnp.sum(
        exchange(grad_part.reshape(groups, 2 * width // groups, hidden), "node").astype(
            jnp.float32
        ),
        axis=0,
    ).astype(jnp.bfloat16)
    grads = exchange(
        jnp.broadcast_to(grad_piece[None], (groups,) + grad_piece.shape), "node"
    ).reshape(2 * width, hidden)
    return (grads[:width], grads[width:], logits)


def solution(mesh):
    in_specs = (
        P("node", "feat"),
        P("node", "feat"),
        P("node", None, None),
        P("node", None),
        P("node"),
        P("node", None),
        P("node"),
        P("feat", None),
        P("feat", None),
        P(),
        P(),
        P("node", None),
    )
    out_specs = (P("feat", None), P("feat", None), P("node", None))
    return jax.shard_map(body, mesh=mesh, in_specs=in_specs, out_specs=out_specs, check_vma=False)
```

```python
import functools

import jax
import jax.numpy as jnp
from jax import lax
from jax.experimental import pallas as pl
from jax.experimental.pallas import tpu as pltpu
from jax.sharding import Mesh
from jax.sharding import PartitionSpec as P

XS = 4
ROW_BLOCK = 256
DEAD = 512.0
PARAMS = pltpu.CompilerParams(vmem_limit_bytes=48 * 1024 * 1024)
NODE = ("x", "z")
FEAT = ("y", "c")


def silu_slope(value):
    gate = jax.nn.sigmoid(value)
    return gate + value * gate * (1.0 - gate)


def dot(a, b, dims=((1,), (0,))):
    return lax.dot_general(a, b, (dims, ((), ())), preferred_element_type=jnp.float32)


def payload_kernel(place_ref, index_ref, count_ref, table_ref, *refs):
    outs, coded = refs[:-1], refs[-1]
    slots, total = index_ref.shape
    nodes = table_ref.shape[0]
    per_x = total // XS
    blocks = per_x // ROW_BLOCK
    index = index_ref[...]
    slot = lax.broadcasted_iota(jnp.int32, (slots, total), 0)
    code = jnp.where(index < 256, index, 255 - index).astype(jnp.float32)
    code = jnp.where(slot < count_ref[...], code, DEAD)
    extra = coded.shape[1] - slots * blocks
    for x in range(XS):
        pieces = [
            code[:, (x * blocks + c) * ROW_BLOCK : (x * blocks + c + 1) * ROW_BLOCK]
            for c in range(blocks)
        ] + [jnp.full((extra, ROW_BLOCK), DEAD, jnp.float32)]
        coded[x] = jnp.concatenate(pieces, axis=0).astype(jnp.bfloat16)
    for shift in range(XS):
        out = outs[shift]
        out[0:nodes, :] = table_ref[...]
        out[nodes:, :] = coded[lax.rem(place_ref[0] + shift, XS)]


def make_payloads(place, index, count, table):
    slots, total = index.shape
    nodes, width = table.shape
    used = slots * (total // XS // ROW_BLOCK)
    extra = -(-used // 16) * 16
    vmem = pl.BlockSpec(memory_space=pltpu.VMEM)
    return pl.pallas_call(
        payload_kernel,
        in_specs=[pl.BlockSpec(memory_space=pltpu.SMEM), vmem, vmem, vmem],
        out_specs=[vmem] * XS,
        out_shape=[jax.ShapeDtypeStruct((nodes + extra, width), jnp.bfloat16)] * XS,
        scratch_shapes=[pltpu.VMEM((XS, extra, ROW_BLOCK), jnp.bfloat16)],
        compiler_params=PARAMS,
        name="payloads",
    )(place, index, count, table)


def gather_kernel(slots, carried, *refs):
    payloads, out_ref = refs[carried:-1], refs[-1]
    blocks = out_ref.shape[0] // ROW_BLOCK
    extra = -(-slots * blocks // 16) * 16
    nodes = payloads[0].shape[0] - extra
    lane = lax.broadcasted_iota(jnp.int32, (ROW_BLOCK, nodes), 1)
    node_code = jnp.where(lane < 256, lane, 255 - lane).astype(jnp.float32).astype(jnp.bfloat16)
    one = jnp.ones((), jnp.bfloat16)
    zero = jnp.zeros((), jnp.bfloat16)
    codes = [ref[nodes:, :].astype(jnp.float32).T.astype(jnp.bfloat16) for ref in payloads]
    for c in range(blocks):
        rows = slice(c * ROW_BLOCK, (c + 1) * ROW_BLOCK)
        total = refs[0][rows, :].astype(jnp.float32) if carried else None
        for ref, code in zip(payloads, codes):
            hits = None
            for k in range(slots):
                column = slots * c + k
                hit = jnp.where(code[:, column : column + 1] == node_code, one, zero)
                hits = hit if hits is None else hits + hit
            part = dot(hits, ref[0:nodes, :])
            total = part if total is None else total + part
        out_ref[rows, :] = total.astype(out_ref.dtype)


def gather_sum(slots, rows, dtype, carried, payloads):
    width = payloads[0].shape[1]
    operands = ([carried] if carried is not None else []) + list(payloads)
    vmem = pl.BlockSpec(memory_space=pltpu.VMEM)
    return pl.pallas_call(
        functools.partial(gather_kernel, slots, int(carried is not None)),
        in_specs=[vmem] * len(operands),
        out_specs=vmem,
        out_shape=jax.ShapeDtypeStruct((rows, width), dtype),
        compiler_params=PARAMS,
        name="gather_sum",
    )(*operands)


def first_kernel(recv_ref, degree_ref, own_ref, self_ref, neigh_ref, mean_ref, out_ref):
    sums = recv_ref[0].astype(jnp.float32)
    for i in range(1, recv_ref.shape[0]):
        sums = sums + recv_ref[i].astype(jnp.float32)
    mean = (sums / degree_ref[...]).astype(jnp.bfloat16)
    mean_ref[...] = mean
    pre = (dot(own_ref[...], self_ref[...]) + dot(mean, neigh_ref[...])).astype(jnp.bfloat16)
    count, height, width = out_ref.shape
    halves = pre.shape[0] // height
    for i in range(count):
        t, h = i // halves, i % halves
        out_ref[i] = pre[h * height : (h + 1) * height, t * width : (t + 1) * width]


def first_layer(recv, degree, own, self_weight, neigh_weight, pieces):
    rows, width = own.shape
    hidden = self_weight.shape[1]
    vmem = pl.BlockSpec(memory_space=pltpu.VMEM)
    return pl.pallas_call(
        first_kernel,
        in_specs=[vmem] * 5,
        out_specs=[vmem] * 2,
        out_shape=[
            jax.ShapeDtypeStruct((rows, width), jnp.bfloat16),
            jax.ShapeDtypeStruct((pieces, rows // 2, 2 * hidden // pieces), jnp.bfloat16),
        ],
        compiler_params=PARAMS,
        name="first_layer",
    )(recv, degree, own, self_weight, neigh_weight)


def second_kernel(pre_ref, adj_ref, inv_ref, two_ref, back_ref, own_ref, mean_ref, hidden_ref, grad_ref):
    count, height, width = pre_ref.shape
    halves = inv_ref.shape[0] // height
    strips = [
        jnp.concatenate([pre_ref[t * halves + h] for h in range(halves)], axis=0)
        for t in range(count // halves)
    ]
    pre = jnp.concatenate(strips, axis=1).astype(jnp.float32)
    gate = jax.nn.sigmoid(pre)
    first_hidden = (pre * gate).astype(jnp.bfloat16)
    slope = (gate + pre * gate * (1.0 - gate)).astype(jnp.bfloat16).astype(jnp.float32)
    adjacency = adj_ref[...]
    inv = inv_ref[...]
    mixed = (dot(adjacency, first_hidden) * inv).astype(jnp.bfloat16)
    pre_two = dot(mixed, two_ref[...])
    gate_two = jax.nn.sigmoid(pre_two)
    hidden_ref[...] = (pre_two * gate_two).astype(jnp.bfloat16)
    slope_two = gate_two + pre_two * gate_two * (1.0 - gate_two)
    grad_two = (back_ref[...] * slope_two).astype(jnp.bfloat16)
    grad_mixed = dot(grad_two, two_ref[...], ((1,), (1,))) * inv
    high = grad_mixed.astype(jnp.bfloat16)
    rest = grad_mixed - high.astype(jnp.float32)
    middle = rest.astype(jnp.bfloat16)
    low = (rest - middle.astype(jnp.float32)).astype(jnp.bfloat16)
    down = ((0,), (0,))
    grad_hidden = dot(adjacency, high, down) + (
        dot(adjacency, middle, down) + dot(adjacency, low, down)
    )
    grad_one = (grad_hidden * slope).astype(jnp.bfloat16)
    width_in = own_ref.shape[1]
    grad_ref[0:width_in, :] = dot(own_ref[...], grad_one, down).astype(jnp.bfloat16)
    grad_ref[width_in:, :] = dot(mean_ref[...], grad_one, down).astype(jnp.bfloat16)


def second_layer(pre, adjacency, inv_count, weight_two, back_two, own, mean):
    rows, width = own.shape
    hidden = weight_two.shape[0]
    vmem = pl.BlockSpec(memory_space=pltpu.VMEM)
    return pl.pallas_call(
        second_kernel,
        in_specs=[vmem] * 7,
        out_specs=[vmem] * 2,
        out_shape=[
            jax.ShapeDtypeStruct((rows, hidden), jnp.bfloat16),
            jax.ShapeDtypeStruct((2 * width, hidden), jnp.bfloat16),
        ],
        compiler_params=PARAMS,
        name="second_layer",
    )(pre, adjacency, inv_count, weight_two, back_two, own, mean)


def spread_kernel(recv_ref, out_ref):
    sums = recv_ref[0].astype(jnp.float32)
    for i in range(1, recv_ref.shape[0]):
        sums = sums + recv_ref[i].astype(jnp.float32)
    piece = sums.astype(jnp.bfloat16)
    for i in range(recv_ref.shape[0]):
        out_ref[i] = piece


def spread(recv):
    vmem = pl.BlockSpec(memory_space=pltpu.VMEM)
    return pl.pallas_call(
        spread_kernel,
        in_specs=[vmem],
        out_specs=vmem,
        out_shape=jax.ShapeDtypeStruct(recv.shape, recv.dtype),
        compiler_params=PARAMS,
        name="sum_and_spread",
    )(recv)


def exchange(pieces, axis):
    return lax.all_to_all(pieces, axis, split_axis=0, concat_axis=0, tiled=True)


def body(
    features,
    own_features,
    neigh_index,
    neigh_count,
    degree,
    local_index,
    local_count,
    self_weight,
    neigh_weight,
    weight_two,
    weight_three,
    cotangent,
):
    groups = lax.axis_size(NODE)
    splits = lax.axis_size(FEAT)
    own_rows, width = own_features.shape
    slots = neigh_index.shape[2]
    per_x = own_rows * (groups // XS)

    place = lax.axis_index("x").reshape(1).astype(jnp.int32)
    payloads = make_payloads(place, neigh_index[0].T, neigh_count, features)
    arrived = [
        lax.ppermute(payloads[s], "x", [(i, (i + s) % XS) for i in range(XS)]) for s in (2, 1, 3)
    ]
    running = gather_sum(slots, per_x, jnp.float32, None, payloads[:1])
    running = gather_sum(slots, per_x, jnp.float32, running, arrived[1:])
    parts = gather_sum(slots, per_x, jnp.bfloat16, running, arrived[:1])
    recv = exchange(parts.reshape(groups // XS, own_rows, width), "z")
    mean_rows, pieces = first_layer(
        recv,
        degree[:, None].astype(jnp.float32),
        own_features,
        self_weight,
        neigh_weight,
        splits,
    )
    pre_piece = jnp.sum(exchange(pieces, FEAT).astype(jnp.float32), axis=0).astype(jnp.bfloat16)
    pre = lax.all_gather(pre_piece, FEAT, axis=0, tiled=False)

    slot_ids = jnp.arange(local_index.shape[1], dtype=jnp.int32)
    live_slots = slot_ids[None, :] < local_count[:, None]
    slot_hits = (
        local_index[:, :, None] == jnp.arange(own_rows, dtype=jnp.int32)[None, None, :]
    ) & live_slots[:, :, None]
    adjacency = (
        jnp.sum(slot_hits.astype(jnp.float32), axis=1) + jnp.eye(own_rows, dtype=jnp.float32)
    ).astype(jnp.bfloat16)
    inv_count = 1.0 / (1.0 + local_count.astype(jnp.float32))
    back_two = dot(cotangent, weight_three, ((1,), (1,)))
    second_hidden, grad_part = second_layer(
        pre, adjacency, inv_count[:, None], weight_two, back_two, own_features, mean_rows
    )
    grad_recv = exchange(grad_part.reshape(groups, -1, grad_part.shape[1]), NODE)
    grads = exchange(spread(grad_recv), NODE).reshape(grad_part.shape)
    logits = dot(second_hidden, weight_three).astype(jnp.bfloat16)
    return (grads[:width], grads[width:], logits)


def solution(mesh):
    nodes, feats = mesh.devices.shape
    fine = Mesh(mesh.devices.reshape(XS, nodes // XS, feats // 2, 2), ("x", "z", "y", "c"))
    in_specs = (
        P(NODE, FEAT),
        P(NODE, FEAT),
        P(NODE, None, None),
        P(NODE, None),
        P(NODE),
        P(NODE, None),
        P(NODE),
        P(FEAT, None),
        P(FEAT, None),
        P(),
        P(),
        P(NODE, None),
    )
    out_specs = (P(FEAT, None), P(FEAT, None), P(NODE, None))
    return jax.shard_map(body, mesh=fine, in_specs=in_specs, out_specs=out_specs, check_vma=False)
```

```python
import functools

import jax
import jax.numpy as jnp
from jax import lax
from jax.experimental import pallas as pl
from jax.experimental.pallas import tpu as pltpu
from jax.sharding import Mesh
from jax.sharding import PartitionSpec as P

XS = 4
ROW_BLOCK = 256
DEAD = 512.0
MIB = 1024 * 1024
NODE = ("x", "z")
FEAT = ("y", "c")


def silu_slope(value):
    gate = jax.nn.sigmoid(value)
    return gate + value * gate * (1.0 - gate)


def params(mib):
    return pltpu.CompilerParams(vmem_limit_bytes=mib * MIB)


def dot(a, b, dims=((1,), (0,))):
    return lax.dot_general(a, b, (dims, ((), ())), preferred_element_type=jnp.float32)


def payload_kernel(place_ref, index_hbm, count_hbm, table_hbm, *refs):
    outs = refs[:XS]
    index_ref, count_ref, table_ref, coded, sems = refs[XS:]
    copies = [
        pltpu.make_async_copy(source, target, sems.at[i])
        for i, (source, target) in enumerate(
            [(index_hbm, index_ref), (count_hbm, count_ref), (table_hbm, table_ref)]
        )
    ]
    for copy in copies:
        copy.start()
    slots, total = index_ref.shape
    nodes = table_ref.shape[0]
    per_x = total // XS
    blocks = per_x // ROW_BLOCK
    copies[0].wait()
    copies[1].wait()
    index = index_ref[...]
    slot = lax.broadcasted_iota(jnp.int32, (slots, total), 0)
    code = jnp.where(index < 256, index, 255 - index).astype(jnp.float32)
    code = jnp.where(slot < count_ref[...], code, DEAD)
    extra = coded.shape[1] - slots * blocks
    for x in range(XS):
        pieces = [
            code[:, (x * blocks + c) * ROW_BLOCK : (x * blocks + c + 1) * ROW_BLOCK]
            for c in range(blocks)
        ] + [jnp.full((extra, ROW_BLOCK), DEAD, jnp.float32)]
        coded[x] = jnp.concatenate(pieces, axis=0).astype(jnp.bfloat16)
    copies[2].wait()
    for shift in range(XS):
        out = outs[shift]
        out[0:nodes, :] = table_ref[...]
        out[nodes:, :] = coded[lax.rem(place_ref[0] + shift, XS)]


def make_payloads(place, index, count, table):
    slots, total = index.shape
    nodes, width = table.shape
    used = slots * (total // XS // ROW_BLOCK)
    extra = -(-used // 16) * 16
    vmem = pl.BlockSpec(memory_space=pltpu.VMEM)
    hbm = pl.BlockSpec(memory_space=pl.ANY)
    return pl.pallas_call(
        payload_kernel,
        in_specs=[pl.BlockSpec(memory_space=pltpu.SMEM), hbm, hbm, hbm],
        out_specs=[vmem] * XS,
        out_shape=[jax.ShapeDtypeStruct((nodes + extra, width), jnp.bfloat16)] * XS,
        scratch_shapes=[
            pltpu.VMEM(index.shape, index.dtype),
            pltpu.VMEM(count.shape, count.dtype),
            pltpu.VMEM(table.shape, table.dtype),
            pltpu.VMEM((XS, extra, ROW_BLOCK), jnp.bfloat16),
            pltpu.SemaphoreType.DMA((3,)),
        ],
        compiler_params=params(60),
        name="payloads",
    )(place, index, count, table)


def gather_kernel(slots, carried, *refs):
    payloads, out_ref = refs[carried:-1], refs[-1]
    blocks = out_ref.shape[0] // ROW_BLOCK
    extra = -(-slots * blocks // 16) * 16
    nodes = payloads[0].shape[0] - extra
    lane = lax.broadcasted_iota(jnp.int32, (ROW_BLOCK, nodes), 1)
    node_code = jnp.where(lane < 256, lane, 255 - lane).astype(jnp.float32).astype(jnp.bfloat16)
    one = jnp.ones((), jnp.bfloat16)
    zero = jnp.zeros((), jnp.bfloat16)
    codes = [ref[nodes:, :].astype(jnp.float32).T.astype(jnp.bfloat16) for ref in payloads]
    for c in range(blocks):
        rows = slice(c * ROW_BLOCK, (c + 1) * ROW_BLOCK)
        total = refs[0][rows, :].astype(jnp.float32) if carried else None
        for ref, code in zip(payloads, codes):
            hits = None
            for k in range(slots):
                column = slots * c + k
                hit = jnp.where(code[:, column : column + 1] == node_code, one, zero)
                hits = hit if hits is None else hits + hit
            part = dot(hits, ref[0:nodes, :])
            total = part if total is None else total + part
        out_ref[rows, :] = total.astype(out_ref.dtype)


def gather_sum(slots, rows, dtype, carried, payloads):
    width = payloads[0].shape[1]
    operands = ([carried] if carried is not None else []) + list(payloads)
    vmem = pl.BlockSpec(memory_space=pltpu.VMEM)
    return pl.pallas_call(
        functools.partial(gather_kernel, slots, int(carried is not None)),
        in_specs=[vmem] * len(operands),
        out_specs=vmem,
        out_shape=jax.ShapeDtypeStruct((rows, width), dtype),
        compiler_params=params(16),
        name="gather_sum",
    )(*operands)


def first_kernel(recv_ref, degree_ref, own_ref, self_ref, neigh_ref, both_ref, out_ref):
    sums = recv_ref[0].astype(jnp.float32)
    for i in range(1, recv_ref.shape[0]):
        sums = sums + recv_ref[i].astype(jnp.float32)
    mean = (sums / degree_ref[...]).astype(jnp.bfloat16)
    width_in = own_ref.shape[1]
    both_ref[:, 0:width_in] = own_ref[...]
    both_ref[:, width_in:] = mean
    pre = (dot(own_ref[...], self_ref[...]) + dot(mean, neigh_ref[...])).astype(jnp.bfloat16)
    count, height, width = out_ref.shape
    halves = pre.shape[0] // height
    for i in range(count):
        t, h = i // halves, i % halves
        out_ref[i] = pre[h * height : (h + 1) * height, t * width : (t + 1) * width]


def first_layer(recv, degree, own, self_weight, neigh_weight, pieces):
    rows, width = own.shape
    hidden = self_weight.shape[1]
    vmem = pl.BlockSpec(memory_space=pltpu.VMEM)
    return pl.pallas_call(
        first_kernel,
        in_specs=[vmem] * 5,
        out_specs=[vmem] * 2,
        out_shape=[
            jax.ShapeDtypeStruct((rows, 2 * width), jnp.bfloat16),
            jax.ShapeDtypeStruct((pieces, rows // 2, 2 * hidden // pieces), jnp.bfloat16),
        ],
        compiler_params=params(16),
        name="first_layer",
    )(recv, degree, own, self_weight, neigh_weight)


def second_kernel(pre_ref, adj_ref, inv_ref, two_ref, back_ref, hidden_ref, grad_ref):
    count, height, width = pre_ref.shape
    halves = inv_ref.shape[0] // height
    strips = [
        jnp.concatenate([pre_ref[t * halves + h] for h in range(halves)], axis=0)
        for t in range(count // halves)
    ]
    pre = jnp.concatenate(strips, axis=1).astype(jnp.float32)
    gate = jax.nn.sigmoid(pre)
    first_hidden = (pre * gate).astype(jnp.bfloat16)
    slope = (gate + pre * gate * (1.0 - gate)).astype(jnp.bfloat16).astype(jnp.float32)
    adjacency = adj_ref[...]
    inv = inv_ref[...]
    mixed = (dot(adjacency, first_hidden) * inv).astype(jnp.bfloat16)
    pre_two = dot(mixed, two_ref[...])
    gate_two = jax.nn.sigmoid(pre_two)
    hidden_ref[...] = (pre_two * gate_two).astype(jnp.bfloat16)
    slope_two = gate_two + pre_two * gate_two * (1.0 - gate_two)
    grad_two = (back_ref[...] * slope_two).astype(jnp.bfloat16)
    grad_mixed = dot(grad_two, two_ref[...], ((1,), (1,))) * inv
    high = grad_mixed.astype(jnp.bfloat16)
    rest = grad_mixed - high.astype(jnp.float32)
    middle = rest.astype(jnp.bfloat16)
    low = (rest - middle.astype(jnp.float32)).astype(jnp.bfloat16)
    down = ((0,), (0,))
    grad_hidden = dot(adjacency, high, down) + (
        dot(adjacency, middle, down) + dot(adjacency, low, down)
    )
    grad_one = (grad_hidden * slope).astype(jnp.bfloat16)
    quarter = grad_ref.shape[2]
    for x in range(grad_ref.shape[0]):
        grad_ref[x] = grad_one[:, x * quarter : (x + 1) * quarter]


def second_layer(pre, adjacency, inv_count, weight_two, back_two):
    rows = adjacency.shape[0]
    hidden = weight_two.shape[0]
    vmem = pl.BlockSpec(memory_space=pltpu.VMEM)
    return pl.pallas_call(
        second_kernel,
        in_specs=[vmem] * 5,
        out_specs=[vmem] * 2,
        out_shape=[
            jax.ShapeDtypeStruct((rows, hidden), jnp.bfloat16),
            jax.ShapeDtypeStruct((XS, rows, hidden // XS), jnp.bfloat16),
        ],
        compiler_params=params(24),
        name="second_layer",
    )(pre, adjacency, inv_count, weight_two, back_two)


def gradient_kernel(both_ref, grad_ref, out_ref):
    rows = grad_ref.shape[1]
    total = None
    for x in range(grad_ref.shape[0]):
        part = dot(both_ref[x * rows : (x + 1) * rows, :], grad_ref[x], ((0,), (0,)))
        total = part if total is None else total + part
    out_ref[...] = total.astype(jnp.bfloat16)


def gradient_part(both, grad):
    vmem = pl.BlockSpec(memory_space=pltpu.VMEM)
    return pl.pallas_call(
        gradient_kernel,
        in_specs=[vmem] * 2,
        out_specs=vmem,
        out_shape=jax.ShapeDtypeStruct((both.shape[1], grad.shape[2]), jnp.bfloat16),
        compiler_params=params(16),
        name="gradient_part",
    )(both, grad)


def spread_kernel(recv_ref, out_ref):
    sums = recv_ref[0].astype(jnp.float32)
    for i in range(1, recv_ref.shape[0]):
        sums = sums + recv_ref[i].astype(jnp.float32)
    piece = sums.astype(jnp.bfloat16)
    for i in range(out_ref.shape[0]):
        out_ref[i] = piece


def spread(recv, copies):
    vmem = pl.BlockSpec(memory_space=pltpu.VMEM)
    return pl.pallas_call(
        spread_kernel,
        in_specs=[vmem],
        out_specs=vmem,
        out_shape=jax.ShapeDtypeStruct((copies,) + recv.shape[1:], recv.dtype),
        compiler_params=params(8),
        name="sum_and_spread",
    )(recv)


def exchange(pieces, axis):
    return lax.all_to_all(pieces, axis, split_axis=0, concat_axis=0, tiled=True)


def body(
    features,
    own_features,
    neigh_index,
    neigh_count,
    degree,
    local_index,
    local_count,
    self_weight,
    neigh_weight,
    weight_two,
    weight_three,
    cotangent,
):
    groups = lax.axis_size(NODE)
    splits = lax.axis_size(FEAT)
    own_rows, width = own_features.shape
    slots = neigh_index.shape[2]
    per_x = own_rows * (groups // XS)

    place = lax.axis_index("x").reshape(1).astype(jnp.int32)
    payloads = make_payloads(place, neigh_index[0].T, neigh_count, features)
    arrived = [
        lax.ppermute(payloads[s], "x", [(i, (i + s) % XS) for i in range(XS)]) for s in (2, 1, 3)
    ]
    running = gather_sum(slots, per_x, jnp.float32, None, payloads[:1])
    running = gather_sum(slots, per_x, jnp.float32, running, arrived[1:])
    parts = gather_sum(slots, per_x, jnp.bfloat16, running, arrived[:1])
    recv = exchange(parts.reshape(groups // XS, own_rows, width), "z")
    both, pieces = first_layer(
        recv,
        degree[:, None].astype(jnp.float32),
        own_features,
        self_weight,
        neigh_weight,
        splits,
    )
    both = lax.all_gather(both, "x", axis=0, tiled=True)
    pre_piece = spread(exchange(pieces, FEAT), 1)
    pre = lax.all_gather(pre_piece, FEAT, axis=0, tiled=True)

    slot_ids = jnp.arange(local_index.shape[1], dtype=jnp.int32)
    live_slots = slot_ids[None, :] < local_count[:, None]
    slot_hits = (
        local_index[:, :, None] == jnp.arange(own_rows, dtype=jnp.int32)[None, None, :]
    ) & live_slots[:, :, None]
    adjacency = (
        jnp.sum(slot_hits.astype(jnp.float32), axis=1) + jnp.eye(own_rows, dtype=jnp.float32)
    ).astype(jnp.bfloat16)
    inv_count = 1.0 / (1.0 + local_count.astype(jnp.float32))
    back_two = dot(cotangent, weight_three, ((1,), (1,)))
    second_hidden, grad_one = second_layer(
        pre, adjacency, inv_count[:, None], weight_two, back_two
    )
    grad_part = gradient_part(both, exchange(grad_one, "x"))
    quarter = grad_part.shape[1]
    grad_recv = exchange(grad_part.reshape(groups // XS, -1, quarter), "z")
    grads = (
        exchange(spread(grad_recv, groups), NODE)
        .reshape(XS, grad_part.shape[0], quarter)
        .transpose(1, 0, 2)
        .reshape(grad_part.shape[0], XS * quarter)
    )
    logits = dot(second_hidden, weight_three).astype(jnp.bfloat16)
    return (grads[:width], grads[width:], logits)


def solution(mesh):
    nodes, feats = mesh.devices.shape
    fine = Mesh(mesh.devices.reshape(XS, nodes // XS, feats // 2, 2), ("x", "z", "y", "c"))
    in_specs = (
        P(NODE, FEAT),
        P(NODE, FEAT),
        P(NODE, None, None),
        P(NODE, None),
        P(NODE),
        P(NODE, None),
        P(NODE),
        P(FEAT, None),
        P(FEAT, None),
        P(),
        P(),
        P(NODE, None),
    )
    out_specs = (P(FEAT, None), P(FEAT, None), P(NODE, None))
    return jax.shard_map(body, mesh=fine, in_specs=in_specs, out_specs=out_specs, check_vma=False)
```

```python
import functools

import jax
import jax.numpy as jnp
from jax import lax
from jax.experimental import pallas as pl
from jax.experimental.pallas import tpu as pltpu
from jax.sharding import Mesh
from jax.sharding import PartitionSpec as P

XS = 4
ROW_BLOCK = 256
DEAD = 512.0
MIB = 1024 * 1024
GATHER_ROWS = 256
NODE = ("x", "z")
FEAT = ("y", "c")


def silu_slope(value):
    gate = jax.nn.sigmoid(value)
    return gate + value * gate * (1.0 - gate)


def params(mib):
    return pltpu.CompilerParams(vmem_limit_bytes=mib * MIB)


def dot(a, b, dims=((1,), (0,))):
    return lax.dot_general(a, b, (dims, ((), ())), preferred_element_type=jnp.float32)


def payload_kernel(place_ref, index_hbm, count_hbm, table_hbm, *refs):
    outs = refs[:XS]
    index_ref, count_ref, table_ref, coded, sems = refs[XS:]
    copies = [
        pltpu.make_async_copy(source, target, sems.at[i])
        for i, (source, target) in enumerate(
            [(index_hbm, index_ref), (count_hbm, count_ref), (table_hbm, table_ref)]
        )
    ]
    for copy in copies:
        copy.start()
    slots, total = index_ref.shape
    nodes = table_ref.shape[0]
    per_x = total // XS
    blocks = per_x // ROW_BLOCK
    copies[0].wait()
    copies[1].wait()
    index = index_ref[...]
    slot = lax.broadcasted_iota(jnp.int32, (slots, total), 0)
    code = jnp.where(index < 256, index, 255 - index).astype(jnp.float32)
    code = jnp.where(slot < count_ref[...], code, DEAD)
    extra = coded.shape[1] - slots * blocks
    for x in range(XS):
        pieces = [
            code[:, (x * blocks + c) * ROW_BLOCK : (x * blocks + c + 1) * ROW_BLOCK]
            for c in range(blocks)
        ] + [jnp.full((extra, ROW_BLOCK), DEAD, jnp.float32)]
        coded[x] = jnp.concatenate(pieces, axis=0).astype(jnp.bfloat16)
    copies[2].wait()
    for shift in range(XS):
        out = outs[shift]
        out[0:nodes, :] = table_ref[...]
        out[nodes:, :] = coded[lax.rem(place_ref[0] + shift, XS)]


def make_payloads(place, index, count, table):
    slots, total = index.shape
    nodes, width = table.shape
    used = slots * (total // XS // ROW_BLOCK)
    extra = -(-used // 16) * 16
    vmem = pl.BlockSpec(memory_space=pltpu.VMEM)
    hbm = pl.BlockSpec(memory_space=pltpu.HBM)
    return pl.pallas_call(
        payload_kernel,
        in_specs=[pl.BlockSpec(memory_space=pltpu.SMEM), hbm, hbm, hbm],
        out_specs=[vmem] * XS,
        out_shape=[jax.ShapeDtypeStruct((nodes + extra, width), jnp.bfloat16)] * XS,
        scratch_shapes=[
            pltpu.VMEM(index.shape, index.dtype),
            pltpu.VMEM(count.shape, count.dtype),
            pltpu.VMEM(table.shape, table.dtype),
            pltpu.VMEM((XS, extra, ROW_BLOCK), jnp.bfloat16),
            pltpu.SemaphoreType.DMA((3,)),
        ],
        compiler_params=params(16),
        name="payloads",
    )(place, index, count, table)


def gather_kernel(slots, carried, *refs):
    payloads, out_ref = refs[carried:-1], refs[-1]
    blocks = out_ref.shape[0] // ROW_BLOCK
    extra = -(-slots * blocks // 16) * 16
    nodes = payloads[0].shape[0] - extra
    lane = lax.broadcasted_iota(jnp.int32, (ROW_BLOCK, nodes), 1)
    node_code = jnp.where(lane < 256, lane, 255 - lane).astype(jnp.float32).astype(jnp.bfloat16)
    one = jnp.ones((), jnp.bfloat16)
    zero = jnp.zeros((), jnp.bfloat16)
    codes = [ref[nodes:, :].astype(jnp.float32).T.astype(jnp.bfloat16) for ref in payloads]
    for c in range(blocks):
        rows = slice(c * ROW_BLOCK, (c + 1) * ROW_BLOCK)
        total = refs[0][rows, :].astype(jnp.float32) if carried else None
        for ref, code in zip(payloads, codes):
            hits = None
            for k in range(slots):
                column = slots * c + k
                hit = jnp.where(code[:, column : column + 1] == node_code, one, zero)
                hits = hit if hits is None else hits + hit
            part = dot(hits, ref[0:nodes, :])
            total = part if total is None else total + part
        out_ref[rows, :] = total.astype(out_ref.dtype)


def gather_sum(slots, rows, dtype, carried, payloads):
    width = payloads[0].shape[1]
    operands = ([carried] if carried is not None else []) + list(payloads)
    vmem = pl.BlockSpec(memory_space=pltpu.VMEM)
    return pl.pallas_call(
        functools.partial(gather_kernel, slots, int(carried is not None)),
        in_specs=[vmem] * len(operands),
        out_specs=vmem,
        out_shape=jax.ShapeDtypeStruct((rows, width), dtype),
        compiler_params=params(16),
        name="gather_sum",
    )(*operands)


def first_kernel(
    recv_ref, degree_ref, own_ref, self_ref, neigh_ref, both_hbm, out_ref, both_ref, sem
):
    sums = recv_ref[0].astype(jnp.float32)
    for i in range(1, recv_ref.shape[0]):
        sums = sums + recv_ref[i].astype(jnp.float32)
    mean = (sums / degree_ref[...]).astype(jnp.bfloat16)
    rows, width_in = own_ref.shape
    both_ref[0:rows, 0:width_in] = own_ref[...]
    both_ref[0:rows, width_in:] = mean
    both_ref[rows:, :] = jnp.zeros((both_ref.shape[0] - rows, 2 * width_in), jnp.bfloat16)
    copy = pltpu.make_async_copy(both_ref, both_hbm, sem)
    copy.start()
    pre = (dot(own_ref[...], self_ref[...]) + dot(mean, neigh_ref[...])).astype(jnp.bfloat16)
    count, height, width = out_ref.shape
    halves = rows // height
    for i in range(count):
        t, h = i // halves, i % halves
        out_ref[i] = pre[h * height : (h + 1) * height, t * width : (t + 1) * width]
    copy.wait()


def first_layer(recv, degree, own, self_weight, neigh_weight, pieces):
    rows, width = own.shape
    hidden = self_weight.shape[1]
    vmem = pl.BlockSpec(memory_space=pltpu.VMEM)
    padded = max(rows, GATHER_ROWS)
    return pl.pallas_call(
        first_kernel,
        in_specs=[vmem] * 5,
        out_specs=[pl.BlockSpec(memory_space=pltpu.HBM), vmem],
        out_shape=[
            jax.ShapeDtypeStruct((padded, 2 * width), jnp.bfloat16),
            jax.ShapeDtypeStruct((pieces, rows // 2, 2 * hidden // pieces), jnp.bfloat16),
        ],
        scratch_shapes=[
            pltpu.VMEM((padded, 2 * width), jnp.bfloat16),
            pltpu.SemaphoreType.DMA(()),
        ],
        compiler_params=params(16),
        name="first_layer",
    )(recv, degree, own, self_weight, neigh_weight)


def pair_kernel(core_ref, pieces_ref, out_ref):
    count = out_ref.shape[0]
    first = core_ref[0] * count
    for i in range(count):
        total = pieces_ref[0, first + i].astype(jnp.float32)
        for source in range(1, pieces_ref.shape[0]):
            total = total + pieces_ref[source, first + i].astype(jnp.float32)
        out_ref[i] = total.astype(jnp.bfloat16)


def pair_sum(core, pieces):
    cores, count, height, width = pieces.shape
    vmem = pl.BlockSpec(memory_space=pltpu.VMEM)
    return pl.pallas_call(
        pair_kernel,
        in_specs=[pl.BlockSpec(memory_space=pltpu.SMEM), vmem],
        out_specs=vmem,
        out_shape=jax.ShapeDtypeStruct((count // cores, height, width), jnp.bfloat16),
        compiler_params=params(8),
        name="pair_sum",
    )(core, pieces)


def second_kernel(
    pre_ref, adj_ref, inv_ref, two_ref, three_ref, back_ref, logits_ref, grad_hbm, grad_ref, sem
):
    count, height, width = pre_ref.shape
    halves = inv_ref.shape[0] // height
    strips = [
        jnp.concatenate([pre_ref[t * halves + h] for h in range(halves)], axis=0)
        for t in range(count // halves)
    ]
    pre = jnp.concatenate(strips, axis=1).astype(jnp.float32)
    gate = jax.nn.sigmoid(pre)
    first_hidden = (pre * gate).astype(jnp.bfloat16)
    slope = (gate + pre * gate * (1.0 - gate)).astype(jnp.bfloat16).astype(jnp.float32)
    adjacency = adj_ref[...]
    inv = inv_ref[...]
    mixed = (dot(adjacency, first_hidden) * inv).astype(jnp.bfloat16)
    pre_two = dot(mixed, two_ref[...])
    gate_two = jax.nn.sigmoid(pre_two)
    second_hidden = (pre_two * gate_two).astype(jnp.bfloat16)
    across = ((1,), (1,))
    logits_ref[...] = dot(three_ref[...], second_hidden, across).astype(jnp.bfloat16)
    slope_two = gate_two + pre_two * gate_two * (1.0 - gate_two)
    grad_two = (back_ref[...] * slope_two).astype(jnp.bfloat16)
    grad_mixed = dot(grad_two, two_ref[...], across) * inv
    high = grad_mixed.astype(jnp.bfloat16)
    rest = grad_mixed - high.astype(jnp.float32)
    middle = rest.astype(jnp.bfloat16)
    low = (rest - middle.astype(jnp.float32)).astype(jnp.bfloat16)
    down = ((0,), (0,))
    grad_hidden = dot(adjacency, high, down) + (
        dot(adjacency, middle, down) + dot(adjacency, low, down)
    )
    grad_one = (grad_hidden * slope).astype(jnp.bfloat16)
    quarter = grad_ref.shape[2]
    for x in range(grad_ref.shape[0]):
        grad_ref[x] = grad_one[:, x * quarter : (x + 1) * quarter]
    copy = pltpu.make_async_copy(grad_ref, grad_hbm, sem)
    copy.start()
    copy.wait()


def second_layer(pre, adjacency, inv_count, weight_two, weight_three, back_two):
    rows = adjacency.shape[0]
    hidden = weight_two.shape[0]
    vmem = pl.BlockSpec(memory_space=pltpu.VMEM)
    return pl.pallas_call(
        second_kernel,
        in_specs=[vmem] * 6,
        out_specs=[vmem, pl.BlockSpec(memory_space=pltpu.HBM)],
        out_shape=[
            jax.ShapeDtypeStruct((weight_three.shape[0], rows), jnp.bfloat16),
            jax.ShapeDtypeStruct((XS, rows, hidden // XS), jnp.bfloat16),
        ],
        scratch_shapes=[
            pltpu.VMEM((XS, rows, hidden // XS), jnp.bfloat16),
            pltpu.SemaphoreType.DMA(()),
        ],
        compiler_params=params(24),
        name="second_layer",
    )(pre, adjacency, inv_count, weight_two, weight_three, back_two)


def gradient_kernel(both_ref, grad_ref, out_ref):
    xs, rows, _ = grad_ref.shape
    padded = both_ref.shape[0] // xs
    total = None
    for x in range(xs):
        part = dot(both_ref[x * padded : x * padded + rows, :], grad_ref[x], ((0,), (0,)))
        total = part if total is None else total + part
    out_ref[...] = total.astype(jnp.bfloat16)


def gradient_part(both, grad):
    vmem = pl.BlockSpec(memory_space=pltpu.VMEM)
    return pl.pallas_call(
        gradient_kernel,
        in_specs=[vmem] * 2,
        out_specs=vmem,
        out_shape=jax.ShapeDtypeStruct((both.shape[1], grad.shape[2]), jnp.bfloat16),
        compiler_params=params(16),
        name="gradient_part",
    )(both, grad)


def spread_kernel(recv_ref, out_ref):
    sums = recv_ref[0].astype(jnp.float32)
    for i in range(1, recv_ref.shape[0]):
        sums = sums + recv_ref[i].astype(jnp.float32)
    piece = sums.astype(jnp.bfloat16)
    for i in range(out_ref.shape[0]):
        out_ref[i] = piece


def spread(recv, copies):
    vmem = pl.BlockSpec(memory_space=pltpu.VMEM)
    return pl.pallas_call(
        spread_kernel,
        in_specs=[vmem],
        out_specs=vmem,
        out_shape=jax.ShapeDtypeStruct((copies,) + recv.shape[1:], recv.dtype),
        compiler_params=params(8),
        name="sum_and_spread",
    )(recv)


def assemble_kernel(recv_hbm, self_hbm, neigh_hbm, sem):
    height, hidden = self_hbm.shape
    width = recv_hbm.shape[1]
    copies = []
    for x in range(hidden // width):
        for i, out in enumerate((self_hbm, neigh_hbm)):
            source = recv_hbm.at[pl.ds((2 * x + i) * height, height), :]
            copies.append(
                pltpu.make_async_copy(source, out.at[:, pl.ds(x * width, width)], sem.at[2 * x + i])
            )
    for copy in copies:
        copy.start()
    for copy in copies:
        copy.wait()


def assemble(recv):
    total, width = recv.shape
    height = total // XS // 2
    shape = jax.ShapeDtypeStruct((height, XS * width), recv.dtype)
    return pl.pallas_call(
        assemble_kernel,
        in_specs=[pl.BlockSpec(memory_space=pl.ANY)],
        out_specs=[pl.BlockSpec(memory_space=pltpu.HBM)] * 2,
        out_shape=[shape] * 2,
        scratch_shapes=[pltpu.SemaphoreType.DMA((2 * XS,))],
        compiler_params=params(8),
        name="assemble",
    )(recv)


def exchange(pieces, axis):
    return lax.all_to_all(pieces, axis, split_axis=0, concat_axis=0, tiled=True)


def body(
    features,
    own_features,
    neigh_index,
    neigh_count,
    degree,
    local_index,
    local_count,
    self_weight,
    neigh_weight,
    weight_two,
    weight_three,
    cotangent,
):
    groups = lax.axis_size(NODE)
    splits = lax.axis_size(FEAT)
    own_rows, width = own_features.shape
    slots = neigh_index.shape[2]
    per_x = own_rows * (groups // XS)

    place = lax.axis_index("x").reshape(1).astype(jnp.int32)
    payloads = make_payloads(place, neigh_index[0].T, neigh_count, features)
    arrived = [
        lax.ppermute(payloads[s], "x", [(i, (i + s) % XS) for i in range(XS)]) for s in (2, 1, 3)
    ]
    running = gather_sum(slots, per_x, jnp.float32, None, payloads[:1])
    running = gather_sum(slots, per_x, jnp.float32, running, arrived[1:])
    parts = gather_sum(slots, per_x, jnp.bfloat16, running, arrived[:1])
    recv = exchange(parts.reshape(groups // XS, own_rows, width), "z")
    both, pieces = first_layer(
        recv,
        degree[:, None].astype(jnp.float32),
        own_features,
        self_weight,
        neigh_weight,
        splits,
    )
    both = lax.all_gather(both, "x", axis=0, tiled=True)
    core = lax.axis_index("c").reshape(1).astype(jnp.int32)
    paired = pair_sum(core, lax.all_gather(pieces, "c", axis=0, tiled=False))
    pre_copies = spread(exchange(paired, "y"), paired.shape[0])
    pre = lax.all_gather(exchange(pre_copies, "y"), "c", axis=0, tiled=True)

    slot_ids = jnp.arange(local_index.shape[1], dtype=jnp.int32)
    live_slots = slot_ids[None, :] < local_count[:, None]
    slot_hits = (
        local_index[:, :, None] == jnp.arange(own_rows, dtype=jnp.int32)[None, None, :]
    ) & live_slots[:, :, None]
    adjacency = (
        jnp.sum(slot_hits.astype(jnp.float32), axis=1) + jnp.eye(own_rows, dtype=jnp.float32)
    ).astype(jnp.bfloat16)
    inv_count = 1.0 / (1.0 + local_count.astype(jnp.float32))
    back_two = dot(cotangent, weight_three, ((1,), (1,)))
    logits, grad_one = second_layer(
        pre, adjacency, inv_count[:, None], weight_two, weight_three.T, back_two
    )
    grad_part = gradient_part(both, exchange(grad_one, "x"))
    quarter = grad_part.shape[1]
    grad_recv = exchange(grad_part.reshape(groups // XS, -1, quarter), "z")
    grads = exchange(spread(grad_recv, groups), NODE)
    grad_self, grad_neigh = assemble(grads.reshape(-1, quarter))
    return (grad_self, grad_neigh, logits.T)


def solution(mesh):
    nodes, feats = mesh.devices.shape
    fine = Mesh(mesh.devices.reshape(XS, nodes // XS, feats // 2, 2), ("x", "z", "y", "c"))
    in_specs = (
        P(NODE, FEAT),
        P(NODE, FEAT),
        P(NODE, None, None),
        P(NODE, None),
        P(NODE),
        P(NODE, None),
        P(NODE),
        P(FEAT, None),
        P(FEAT, None),
        P(),
        P(),
        P(NODE, None),
    )
    out_specs = (P(FEAT, None), P(FEAT, None), P(NODE, None))
    return jax.shard_map(body, mesh=fine, in_specs=in_specs, out_specs=out_specs, check_vma=False)
```

```python
import functools

import jax
import jax.numpy as jnp
from jax import lax
from jax.experimental import pallas as pl
from jax.experimental.pallas import tpu as pltpu
from jax.sharding import Mesh
from jax.sharding import PartitionSpec as P

XS = 4
ROW_BLOCK = 256
DEAD = 512.0
MIB = 1024 * 1024
NODE = ("x", "z")
FEAT = ("y", "c")


def silu_slope(value):
    gate = jax.nn.sigmoid(value)
    return gate + value * gate * (1.0 - gate)


def params(mib):
    return pltpu.CompilerParams(vmem_limit_bytes=mib * MIB)


def dot(a, b, dims=((1,), (0,))):
    return lax.dot_general(a, b, (dims, ((), ())), preferred_element_type=jnp.float32)


def payload_kernel(place_ref, index_hbm, count_hbm, table_hbm, *refs):
    outs = refs[:XS]
    index_ref, count_ref, table_ref, coded, sems = refs[XS:]
    nodes = table_hbm.shape[0]
    first = pltpu.make_async_copy(index_hbm, index_ref, sems.at[0])
    second = pltpu.make_async_copy(count_hbm, count_ref, sems.at[1])
    third = pltpu.make_async_copy(table_hbm, table_ref, sems.at[2 + 2 * XS])
    first.start()
    second.start()
    third.start()
    slots, total = index_ref.shape
    blocks = total // XS // ROW_BLOCK
    extra = coded.shape[1] - slots * blocks
    first.wait()
    second.wait()
    index = index_ref[...]
    slot = lax.broadcasted_iota(jnp.int32, (slots, total), 0)
    code = jnp.where(index < 256, index, 255 - index).astype(jnp.float32)
    code = jnp.where(slot < count_ref[...], code, DEAD)
    for x in range(XS):
        pieces = [
            code[:, (x * blocks + c) * ROW_BLOCK : (x * blocks + c + 1) * ROW_BLOCK]
            for c in range(blocks)
        ] + [jnp.full((extra, ROW_BLOCK), DEAD, jnp.float32)]
        coded[x] = jnp.concatenate(pieces, axis=0).astype(jnp.bfloat16)
    third.wait()
    copies = []
    for shift in range(XS):
        target = outs[shift].at[pl.ds(0, nodes), :]
        copies.append(pltpu.make_async_copy(table_ref, target, sems.at[2 + shift]))
        copies[shift].start()
    for shift in range(XS):
        source = coded.at[lax.rem(place_ref[0] + shift, XS)]
        target = outs[shift].at[pl.ds(nodes, coded.shape[1]), :]
        copies.append(pltpu.make_async_copy(source, target, sems.at[2 + XS + shift]))
        copies[XS + shift].start()
    for copy in copies:
        copy.wait()


def make_payloads(place, index, count, table):
    slots, total = index.shape
    nodes, width = table.shape
    used = slots * (total // XS // ROW_BLOCK)
    extra = -(-used // 16) * 16
    hbm = pl.BlockSpec(memory_space=pltpu.HBM)
    return pl.pallas_call(
        payload_kernel,
        in_specs=[pl.BlockSpec(memory_space=pltpu.SMEM), hbm, hbm, hbm],
        out_specs=[hbm] * XS,
        out_shape=[jax.ShapeDtypeStruct((nodes + extra, width), jnp.bfloat16)] * XS,
        scratch_shapes=[
            pltpu.VMEM(index.shape, index.dtype),
            pltpu.VMEM(count.shape, count.dtype),
            pltpu.VMEM(table.shape, table.dtype),
            pltpu.VMEM((XS, extra, ROW_BLOCK), jnp.bfloat16),
            pltpu.SemaphoreType.DMA((3 + 2 * XS,)),
        ],
        compiler_params=params(60),
        name="payloads",
    )(place, index, count, table)


def gather_kernel(slots, carried, *refs):
    payloads, out_ref = refs[carried:-1], refs[-1]
    blocks = out_ref.shape[0] // ROW_BLOCK
    extra = -(-slots * blocks // 16) * 16
    nodes = payloads[0].shape[0] - extra
    lane = lax.broadcasted_iota(jnp.int32, (ROW_BLOCK, nodes), 1)
    node_code = jnp.where(lane < 256, lane, 255 - lane).astype(jnp.float32).astype(jnp.bfloat16)
    one = jnp.ones((), jnp.bfloat16)
    zero = jnp.zeros((), jnp.bfloat16)
    codes = [ref[nodes:, :].astype(jnp.float32).T.astype(jnp.bfloat16) for ref in payloads]
    for c in range(blocks):
        rows = slice(c * ROW_BLOCK, (c + 1) * ROW_BLOCK)
        total = refs[0][rows, :].astype(jnp.float32) if carried else None
        for ref, code in zip(payloads, codes):
            hits = None
            for k in range(slots):
                column = slots * c + k
                hit = jnp.where(code[:, column : column + 1] == node_code, one, zero)
                hits = hit if hits is None else hits + hit
            part = dot(hits, ref[0:nodes, :])
            total = part if total is None else total + part
        out_ref[rows, :] = total.astype(out_ref.dtype)


def gather_sum(slots, rows, dtype, carried, payloads):
    width = payloads[0].shape[1]
    operands = ([carried] if carried is not None else []) + list(payloads)
    vmem = pl.BlockSpec(memory_space=pltpu.VMEM)
    return pl.pallas_call(
        functools.partial(gather_kernel, slots, int(carried is not None)),
        in_specs=[vmem] * len(operands),
        out_specs=vmem,
        out_shape=jax.ShapeDtypeStruct((rows, width), dtype),
        compiler_params=params(16),
        name="gather_sum",
    )(*operands)


def first_kernel(recv_ref, degree_ref, own_ref, self_ref, neigh_ref, mean_ref, out_ref):
    sums = recv_ref[0].astype(jnp.float32)
    for i in range(1, recv_ref.shape[0]):
        sums = sums + recv_ref[i].astype(jnp.float32)
    mean = (sums / degree_ref[...]).astype(jnp.bfloat16)
    mean_ref[...] = mean
    pre = (dot(own_ref[...], self_ref[...]) + dot(mean, neigh_ref[...])).astype(jnp.bfloat16)
    count, height, width = out_ref.shape
    halves = pre.shape[0] // height
    for i in range(count):
        t, h = i // halves, i % halves
        out_ref[i] = pre[h * height : (h + 1) * height, t * width : (t + 1) * width]


def first_layer(recv, degree, own, self_weight, neigh_weight, pieces):
    rows, width = own.shape
    hidden = self_weight.shape[1]
    vmem = pl.BlockSpec(memory_space=pltpu.VMEM)
    return pl.pallas_call(
        first_kernel,
        in_specs=[vmem] * 5,
        out_specs=[vmem] * 2,
        out_shape=[
            jax.ShapeDtypeStruct((rows, width), jnp.bfloat16),
            jax.ShapeDtypeStruct((pieces, rows // 2, 2 * hidden // pieces), jnp.bfloat16),
        ],
        compiler_params=params(16),
        name="first_layer",
    )(recv, degree, own, self_weight, neigh_weight)


def pair_kernel(core_ref, pieces_ref, out_ref):
    count = out_ref.shape[0]
    first = core_ref[0] * count
    for i in range(count):
        total = pieces_ref[0, first + i].astype(jnp.float32)
        for source in range(1, pieces_ref.shape[0]):
            total = total + pieces_ref[source, first + i].astype(jnp.float32)
        out_ref[i] = total.astype(jnp.bfloat16)


def pair_sum(core, pieces):
    cores, count, height, width = pieces.shape
    vmem = pl.BlockSpec(memory_space=pltpu.VMEM)
    return pl.pallas_call(
        pair_kernel,
        in_specs=[pl.BlockSpec(memory_space=pltpu.SMEM), vmem],
        out_specs=vmem,
        out_shape=jax.ShapeDtypeStruct((count // cores, height, width), jnp.bfloat16),
        compiler_params=params(8),
        name="pair_sum",
    )(core, pieces)


def second_kernel(
    pre_ref, adj_ref, inv_ref, two_ref, three_ref, back_ref, logits_ref, grad_hbm, grad_ref, sem
):
    count, height, width = pre_ref.shape
    halves = inv_ref.shape[0] // height
    strips = [
        jnp.concatenate([pre_ref[t * halves + h] for h in range(halves)], axis=0)
        for t in range(count // halves)
    ]
    pre = jnp.concatenate(strips, axis=1).astype(jnp.float32)
    gate = jax.nn.sigmoid(pre)
    first_hidden = (pre * gate).astype(jnp.bfloat16)
    slope = (gate + pre * gate * (1.0 - gate)).astype(jnp.bfloat16).astype(jnp.float32)
    adjacency = adj_ref[...]
    inv = inv_ref[...]
    mixed = (dot(adjacency, first_hidden) * inv).astype(jnp.bfloat16)
    pre_two = dot(mixed, two_ref[...])
    gate_two = jax.nn.sigmoid(pre_two)
    second_hidden = (pre_two * gate_two).astype(jnp.bfloat16)
    across = ((1,), (1,))
    logits_ref[...] = dot(three_ref[...], second_hidden, across).astype(jnp.bfloat16)
    slope_two = gate_two + pre_two * gate_two * (1.0 - gate_two)
    grad_two = (back_ref[...] * slope_two).astype(jnp.bfloat16)
    grad_mixed = dot(grad_two, two_ref[...], across) * inv
    high = grad_mixed.astype(jnp.bfloat16)
    rest = grad_mixed - high.astype(jnp.float32)
    middle = rest.astype(jnp.bfloat16)
    low = (rest - middle.astype(jnp.float32)).astype(jnp.bfloat16)
    down = ((0,), (0,))
    grad_hidden = dot(adjacency, high, down) + (
        dot(adjacency, middle, down) + dot(adjacency, low, down)
    )
    grad_one = (grad_hidden * slope).astype(jnp.bfloat16)
    quarter = grad_ref.shape[2]
    for x in range(grad_ref.shape[0]):
        grad_ref[x] = grad_one[:, x * quarter : (x + 1) * quarter]
    copy = pltpu.make_async_copy(grad_ref, grad_hbm, sem)
    copy.start()
    copy.wait()


def second_layer(pre, adjacency, inv_count, weight_two, weight_three, back_two):
    rows = adjacency.shape[0]
    hidden = weight_two.shape[0]
    vmem = pl.BlockSpec(memory_space=pltpu.VMEM)
    return pl.pallas_call(
        second_kernel,
        in_specs=[vmem] * 6,
        out_specs=[vmem, pl.BlockSpec(memory_space=pltpu.HBM)],
        out_shape=[
            jax.ShapeDtypeStruct((weight_three.shape[0], rows), jnp.bfloat16),
            jax.ShapeDtypeStruct((XS, rows, hidden // XS), jnp.bfloat16),
        ],
        scratch_shapes=[
            pltpu.VMEM((XS, rows, hidden // XS), jnp.bfloat16),
            pltpu.SemaphoreType.DMA(()),
        ],
        compiler_params=params(24),
        name="second_layer",
    )(pre, adjacency, inv_count, weight_two, weight_three, back_two)


def gradient_kernel(place_ref, *refs):
    operands, grad_ref, out_ref = refs[:-2], refs[-2], refs[-1]
    width = operands[0].shape[1]
    for half in range(2):
        total = None
        for shift in range(XS):
            source = lax.rem(place_ref[0] + (XS - shift), XS)
            rows = operands[half * XS + shift][...]
            part = dot(rows, grad_ref[source], ((0,), (0,)))
            total = part if total is None else total + part
        out_ref[half * width : (half + 1) * width, :] = total.astype(jnp.bfloat16)


def gradient_part(place, own, mean, grad):
    vmem = pl.BlockSpec(memory_space=pltpu.VMEM)
    return pl.pallas_call(
        gradient_kernel,
        in_specs=[pl.BlockSpec(memory_space=pltpu.SMEM)] + [vmem] * (2 * XS + 1),
        out_specs=vmem,
        out_shape=jax.ShapeDtypeStruct((2 * own[0].shape[1], grad.shape[2]), jnp.bfloat16),
        compiler_params=params(16),
        name="gradient_part",
    )(place, *own, *mean, grad)


def spread_kernel(recv_ref, out_ref):
    sums = recv_ref[0].astype(jnp.float32)
    for i in range(1, recv_ref.shape[0]):
        sums = sums + recv_ref[i].astype(jnp.float32)
    piece = sums.astype(jnp.bfloat16)
    for i in range(out_ref.shape[0]):
        out_ref[i] = piece


def spread(recv, copies):
    vmem = pl.BlockSpec(memory_space=pltpu.VMEM)
    return pl.pallas_call(
        spread_kernel,
        in_specs=[vmem],
        out_specs=vmem,
        out_shape=jax.ShapeDtypeStruct((copies,) + recv.shape[1:], recv.dtype),
        compiler_params=params(8),
        name="sum_and_spread",
    )(recv)


def assemble_kernel(recv_hbm, self_hbm, neigh_hbm, sem):
    height, hidden = self_hbm.shape
    width = recv_hbm.shape[1]
    copies = []
    for x in range(hidden // width):
        for i, out in enumerate((self_hbm, neigh_hbm)):
            source = recv_hbm.at[pl.ds((2 * x + i) * height, height), :]
            copies.append(
                pltpu.make_async_copy(source, out.at[:, pl.ds(x * width, width)], sem.at[2 * x + i])
            )
    for copy in copies:
        copy.start()
    for copy in copies:
        copy.wait()


def assemble(recv):
    total, width = recv.shape
    height = total // XS // 2
    shape = jax.ShapeDtypeStruct((height, XS * width), recv.dtype)
    return pl.pallas_call(
        assemble_kernel,
        in_specs=[pl.BlockSpec(memory_space=pl.ANY)],
        out_specs=[pl.BlockSpec(memory_space=pltpu.HBM)] * 2,
        out_shape=[shape] * 2,
        scratch_shapes=[pltpu.SemaphoreType.DMA((2 * XS,))],
        compiler_params=params(8),
        name="assemble",
    )(recv)


def exchange(pieces, axis):
    return lax.all_to_all(pieces, axis, split_axis=0, concat_axis=0, tiled=True)


def shift_x(array, steps):
    return lax.ppermute(array, "x", [(i, (i + steps) % XS) for i in range(XS)])


def body(
    features,
    own_features,
    neigh_index,
    neigh_count,
    degree,
    local_index,
    local_count,
    self_weight,
    neigh_weight,
    weight_two,
    weight_three,
    cotangent,
):
    groups = lax.axis_size(NODE)
    splits = lax.axis_size(FEAT)
    own_rows, width = own_features.shape
    slots = neigh_index.shape[2]
    per_x = own_rows * (groups // XS)

    place = lax.axis_index("x").reshape(1).astype(jnp.int32)
    payloads = make_payloads(place, neigh_index[0].T, neigh_count, features)
    arrived = [shift_x(payloads[s], s) for s in (2, 1, 3)]
    running = gather_sum(slots, per_x, jnp.float32, None, payloads[:1])
    running = gather_sum(slots, per_x, jnp.float32, running, arrived[1:])
    parts = gather_sum(slots, per_x, jnp.bfloat16, running, arrived[:1])
    parts, own_late = lax.optimization_barrier((parts, own_features))
    own = [shift_x(own_late, s) for s in range(1, XS)]
    recv = exchange(parts.reshape(groups // XS, own_rows, width), "z")
    recv, *own = lax.optimization_barrier((recv, *own))
    mean_rows, pieces = first_layer(
        recv,
        degree[:, None].astype(jnp.float32),
        own_features,
        self_weight,
        neigh_weight,
        splits,
    )
    mean = [shift_x(mean_rows, s) for s in range(1, XS)]
    core = lax.axis_index("c").reshape(1).astype(jnp.int32)
    paired = pair_sum(core, lax.all_gather(pieces, "c", axis=0, tiled=False))
    paired, mean[0], mean[2] = lax.optimization_barrier((exchange(paired, "y"), mean[0], mean[2]))
    pre_copies = spread(paired, paired.shape[0])
    pre, mean[1] = lax.optimization_barrier((exchange(pre_copies, "y"), mean[1]))
    pre = lax.all_gather(pre, "c", axis=0, tiled=True)

    slot_ids = jnp.arange(local_index.shape[1], dtype=jnp.int32)
    live_slots = slot_ids[None, :] < local_count[:, None]
    slot_hits = (
        local_index[:, :, None] == jnp.arange(own_rows, dtype=jnp.int32)[None, None, :]
    ) & live_slots[:, :, None]
    adjacency = (
        jnp.sum(slot_hits.astype(jnp.float32), axis=1) + jnp.eye(own_rows, dtype=jnp.float32)
    ).astype(jnp.bfloat16)
    inv_count = 1.0 / (1.0 + local_count.astype(jnp.float32))
    back_two = dot(cotangent, weight_three, ((1,), (1,)))
    logits, grad_one = second_layer(
        pre, adjacency, inv_count[:, None], weight_two, weight_three.T, back_two
    )
    grad_part = gradient_part(place, [own_features] + own, [mean_rows] + mean, exchange(grad_one, "x"))
    quarter = grad_part.shape[1]
    grad_recv = exchange(grad_part.reshape(groups // XS, -1, quarter), "z")
    grads = exchange(spread(grad_recv, groups), NODE)
    grad_self, grad_neigh = assemble(grads.reshape(-1, quarter))
    return (grad_self, grad_neigh, logits.T)


def solution(mesh):
    nodes, feats = mesh.devices.shape
    fine = Mesh(mesh.devices.reshape(XS, nodes // XS, feats // 2, 2), ("x", "z", "y", "c"))
    in_specs = (
        P(NODE, FEAT),
        P(NODE, FEAT),
        P(NODE, None, None),
        P(NODE, None),
        P(NODE),
        P(NODE, None),
        P(NODE),
        P(FEAT, None),
        P(FEAT, None),
        P(),
        P(),
        P(NODE, None),
    )
    out_specs = (P(FEAT, None), P(FEAT, None), P(NODE, None))
    return jax.shard_map(body, mesh=fine, in_specs=in_specs, out_specs=out_specs, check_vma=False)
```

```python
import functools

import jax
import jax.numpy as jnp
from jax import lax
from jax.experimental import pallas as pl
from jax.experimental.pallas import tpu as pltpu
from jax.sharding import Mesh
from jax.sharding import PartitionSpec as P

XS = 4
ROW_BLOCK = 256
DEAD = 512.0
MIB = 1024 * 1024
NODE = ("x", "z")
FEAT = ("y", "c")


def silu_slope(value):
    gate = jax.nn.sigmoid(value)
    return gate + value * gate * (1.0 - gate)


def params(mib):
    return pltpu.CompilerParams(vmem_limit_bytes=mib * MIB)


def dot(a, b, dims=((1,), (0,))):
    return lax.dot_general(a, b, (dims, ((), ())), preferred_element_type=jnp.float32)


def payload_kernel(place_ref, index_hbm, count_hbm, table_hbm, *refs):
    outs = refs[:XS]
    index_ref, count_ref, table_ref, coded, sems = refs[XS:]
    nodes = table_hbm.shape[0]
    first = pltpu.make_async_copy(index_hbm, index_ref, sems.at[0])
    second = pltpu.make_async_copy(count_hbm, count_ref, sems.at[1])
    third = pltpu.make_async_copy(table_hbm, table_ref, sems.at[2 + 2 * XS])
    first.start()
    second.start()
    third.start()
    slots, total = index_ref.shape
    blocks = total // XS // ROW_BLOCK
    extra = coded.shape[1] - slots * blocks
    first.wait()
    second.wait()
    index = index_ref[...]
    slot = lax.broadcasted_iota(jnp.int32, (slots, total), 0)
    code = jnp.where(index < 256, index, 255 - index).astype(jnp.float32)
    code = jnp.where(slot < count_ref[...], code, DEAD)
    for x in range(XS):
        pieces = [
            code[:, (x * blocks + c) * ROW_BLOCK : (x * blocks + c + 1) * ROW_BLOCK]
            for c in range(blocks)
        ] + [jnp.full((extra, ROW_BLOCK), DEAD, jnp.float32)]
        coded[x] = jnp.concatenate(pieces, axis=0).astype(jnp.bfloat16)
    third.wait()
    copies = []
    for shift in range(XS):
        target = outs[shift].at[pl.ds(0, nodes), :]
        copies.append(pltpu.make_async_copy(table_ref, target, sems.at[2 + shift]))
        copies[shift].start()
    for shift in range(XS):
        source = coded.at[lax.rem(place_ref[0] + shift, XS)]
        target = outs[shift].at[pl.ds(nodes, coded.shape[1]), :]
        copies.append(pltpu.make_async_copy(source, target, sems.at[2 + XS + shift]))
        copies[XS + shift].start()
    for copy in copies:
        copy.wait()


def make_payloads(place, index, count, table):
    slots, total = index.shape
    nodes, width = table.shape
    used = slots * (total // XS // ROW_BLOCK)
    extra = -(-used // 16) * 16
    hbm = pl.BlockSpec(memory_space=pltpu.HBM)
    return pl.pallas_call(
        payload_kernel,
        in_specs=[pl.BlockSpec(memory_space=pltpu.SMEM), hbm, hbm, hbm],
        out_specs=[hbm] * XS,
        out_shape=[jax.ShapeDtypeStruct((nodes + extra, width), jnp.bfloat16)] * XS,
        scratch_shapes=[
            pltpu.VMEM(index.shape, index.dtype),
            pltpu.VMEM(count.shape, count.dtype),
            pltpu.VMEM(table.shape, table.dtype),
            pltpu.VMEM((XS, extra, ROW_BLOCK), jnp.bfloat16),
            pltpu.SemaphoreType.DMA((3 + 2 * XS,)),
        ],
        compiler_params=params(16),
        name="payloads",
    )(place, index, count, table)


def gather_kernel(slots, carried, staged, *refs):
    if staged:
        *refs, out_hbm, out_ref, sems = refs
        copies = []
    else:
        *refs, out_ref = refs
    payloads = refs[carried:]
    blocks = out_ref.shape[0] // ROW_BLOCK
    extra = -(-slots * blocks // 16) * 16
    nodes = payloads[0].shape[0] - extra
    lane = lax.broadcasted_iota(jnp.int32, (ROW_BLOCK, nodes), 1)
    node_code = jnp.where(lane < 256, lane, 255 - lane).astype(jnp.float32).astype(jnp.bfloat16)
    one = jnp.ones((), jnp.bfloat16)
    zero = jnp.zeros((), jnp.bfloat16)
    codes = [ref[nodes:, :].astype(jnp.float32).T.astype(jnp.bfloat16) for ref in payloads]
    for c in range(blocks):
        rows = slice(c * ROW_BLOCK, (c + 1) * ROW_BLOCK)
        total = refs[0][rows, :].astype(jnp.float32) if carried else None
        for ref, code in zip(payloads, codes):
            hits = None
            for k in range(slots):
                column = slots * c + k
                hit = jnp.where(code[:, column : column + 1] == node_code, one, zero)
                hits = hit if hits is None else hits + hit
            part = dot(hits, ref[0:nodes, :])
            total = part if total is None else total + part
        out_ref[rows, :] = total.astype(out_ref.dtype)
        if staged:
            block = pl.ds(c * ROW_BLOCK, ROW_BLOCK)
            copies.append(pltpu.make_async_copy(out_ref.at[block], out_hbm.at[block], sems.at[c]))
            copies[c].start()
    if staged:
        for copy in copies:
            copy.wait()


def gather_sum(slots, rows, dtype, carried, payloads, staged=False):
    width = payloads[0].shape[1]
    operands = ([carried] if carried is not None else []) + list(payloads)
    vmem = pl.BlockSpec(memory_space=pltpu.VMEM)
    return pl.pallas_call(
        functools.partial(gather_kernel, slots, int(carried is not None), staged),
        in_specs=[vmem] * len(operands),
        out_specs=pl.BlockSpec(memory_space=pl.ANY) if staged else vmem,
        out_shape=jax.ShapeDtypeStruct((rows, width), dtype),
        scratch_shapes=[
            pltpu.VMEM((rows, width), dtype),
            pltpu.SemaphoreType.DMA((rows // ROW_BLOCK,)),
        ]
        if staged
        else [],
        compiler_params=params(16),
        name="gather_sum",
    )(*operands)


def first_kernel(recv_ref, degree_ref, own_ref, self_ref, neigh_ref, mean_ref, out_ref):
    sums = recv_ref[0].astype(jnp.float32)
    for i in range(1, recv_ref.shape[0]):
        sums = sums + recv_ref[i].astype(jnp.float32)
    mean = (sums / degree_ref[...]).astype(jnp.bfloat16)
    mean_ref[...] = mean
    pre = (dot(own_ref[...], self_ref[...]) + dot(mean, neigh_ref[...])).astype(jnp.bfloat16)
    count, height, width = out_ref.shape
    halves = pre.shape[0] // height
    for i in range(count):
        t, h = i // halves, i % halves
        out_ref[i] = pre[h * height : (h + 1) * height, t * width : (t + 1) * width]


def first_layer(recv, degree, own, self_weight, neigh_weight, pieces):
    rows, width = own.shape
    hidden = self_weight.shape[1]
    vmem = pl.BlockSpec(memory_space=pltpu.VMEM)
    return pl.pallas_call(
        first_kernel,
        in_specs=[vmem] * 5,
        out_specs=[vmem] * 2,
        out_shape=[
            jax.ShapeDtypeStruct((rows, width), jnp.bfloat16),
            jax.ShapeDtypeStruct((pieces, rows // 2, 2 * hidden // pieces), jnp.bfloat16),
        ],
        compiler_params=params(16),
        name="first_layer",
    )(recv, degree, own, self_weight, neigh_weight)


def pair_kernel(core_ref, pieces_ref, out_ref):
    count = out_ref.shape[0]
    first = core_ref[0] * count
    for i in range(count):
        total = pieces_ref[0, first + i].astype(jnp.float32)
        for source in range(1, pieces_ref.shape[0]):
            total = total + pieces_ref[source, first + i].astype(jnp.float32)
        out_ref[i] = total.astype(jnp.bfloat16)


def pair_sum(core, pieces):
    cores, count, height, width = pieces.shape
    vmem = pl.BlockSpec(memory_space=pltpu.VMEM)
    return pl.pallas_call(
        pair_kernel,
        in_specs=[pl.BlockSpec(memory_space=pltpu.SMEM), vmem],
        out_specs=vmem,
        out_shape=jax.ShapeDtypeStruct((count // cores, height, width), jnp.bfloat16),
        compiler_params=params(8),
        name="pair_sum",
    )(core, pieces)


def second_kernel(
    pre_ref, adj_ref, two_ref, three_ref, cot_ref, logits_out, grad_ref, logits_ref, sem
):
    count, height, width = pre_ref.shape
    halves = adj_ref.shape[0] // height
    strips = [
        jnp.concatenate([pre_ref[t * halves + h] for h in range(halves)], axis=0)
        for t in range(count // halves)
    ]
    pre = jnp.concatenate(strips, axis=1).astype(jnp.float32)
    gate = jax.nn.sigmoid(pre)
    first_hidden = (pre * gate).astype(jnp.bfloat16)
    slope = (gate + pre * gate * (1.0 - gate)).astype(jnp.bfloat16).astype(jnp.float32)
    adjacency = adj_ref[...]
    inv = 1.0 / jnp.sum(adjacency.astype(jnp.float32), axis=1, keepdims=True)
    mixed = (dot(adjacency, first_hidden) * inv).astype(jnp.bfloat16)
    pre_two = dot(mixed, two_ref[...])
    gate_two = jax.nn.sigmoid(pre_two)
    second_hidden = (pre_two * gate_two).astype(jnp.bfloat16)
    across = ((1,), (1,))
    logits_ref[...] = dot(three_ref[...], second_hidden, across).astype(jnp.bfloat16)
    copy = pltpu.make_async_copy(logits_ref, logits_out, sem)
    copy.start()
    slope_two = gate_two + pre_two * gate_two * (1.0 - gate_two)
    back_two = dot(cot_ref[...], three_ref[...], ((0,), (0,)))
    grad_two = (back_two * slope_two).astype(jnp.bfloat16)
    grad_mixed = dot(grad_two, two_ref[...], across) * inv
    high = grad_mixed.astype(jnp.bfloat16)
    rest = grad_mixed - high.astype(jnp.float32)
    middle = rest.astype(jnp.bfloat16)
    low = (rest - middle.astype(jnp.float32)).astype(jnp.bfloat16)
    down = ((0,), (0,))
    grad_hidden = dot(adjacency, high, down) + (
        dot(adjacency, middle, down) + dot(adjacency, low, down)
    )
    grad_one = (grad_hidden * slope).astype(jnp.bfloat16)
    quarter = grad_ref.shape[2]
    for x in range(grad_ref.shape[0]):
        grad_ref[x] = grad_one[:, x * quarter : (x + 1) * quarter]
    copy.wait()


def second_layer(pre, adjacency, weight_two, weight_three, cotangent):
    rows = adjacency.shape[0]
    hidden = weight_two.shape[0]
    classes = weight_three.shape[0]
    vmem = pl.BlockSpec(memory_space=pltpu.VMEM)
    return pl.pallas_call(
        second_kernel,
        in_specs=[vmem] * 5,
        out_specs=[pl.BlockSpec(memory_space=pl.ANY), vmem],
        out_shape=[
            jax.ShapeDtypeStruct((classes, rows), jnp.bfloat16),
            jax.ShapeDtypeStruct((XS, rows, hidden // XS), jnp.bfloat16),
        ],
        scratch_shapes=[
            pltpu.VMEM((classes, rows), jnp.bfloat16),
            pltpu.SemaphoreType.DMA(()),
        ],
        compiler_params=params(24),
        name="second_layer",
    )(pre, adjacency, weight_two, weight_three, cotangent)


def gradient_kernel(place_ref, *refs):
    operands, grad_ref, out_ref = refs[:-2], refs[-2], refs[-1]
    width = operands[0].shape[1]
    for half in range(2):
        total = None
        for shift in range(XS):
            source = lax.rem(place_ref[0] + (XS - shift), XS)
            rows = operands[half * XS + shift][...]
            part = dot(rows, grad_ref[source], ((0,), (0,)))
            total = part if total is None else total + part
        out_ref[half * width : (half + 1) * width, :] = total.astype(jnp.bfloat16)


def gradient_part(place, own, mean, grad):
    vmem = pl.BlockSpec(memory_space=pltpu.VMEM)
    return pl.pallas_call(
        gradient_kernel,
        in_specs=[pl.BlockSpec(memory_space=pltpu.SMEM)] + [vmem] * (2 * XS + 1),
        out_specs=vmem,
        out_shape=jax.ShapeDtypeStruct((2 * own[0].shape[1], grad.shape[2]), jnp.bfloat16),
        compiler_params=params(16),
        name="gradient_part",
    )(place, *own, *mean, grad)


def spread_kernel(recv_ref, out_ref):
    sums = recv_ref[0].astype(jnp.float32)
    for i in range(1, recv_ref.shape[0]):
        sums = sums + recv_ref[i].astype(jnp.float32)
    piece = sums.astype(jnp.bfloat16)
    for i in range(out_ref.shape[0]):
        out_ref[i] = piece


def spread(recv, copies):
    vmem = pl.BlockSpec(memory_space=pltpu.VMEM)
    return pl.pallas_call(
        spread_kernel,
        in_specs=[vmem],
        out_specs=vmem,
        out_shape=jax.ShapeDtypeStruct((copies,) + recv.shape[1:], recv.dtype),
        compiler_params=params(8),
        name="sum_and_spread",
    )(recv)


def assemble_kernel(recv_hbm, self_hbm, neigh_hbm, sem):
    height, hidden = self_hbm.shape
    width = recv_hbm.shape[1]
    copies = []
    for x in range(hidden // width):
        for i, out in enumerate((self_hbm, neigh_hbm)):
            source = recv_hbm.at[pl.ds((2 * x + i) * height, height), :]
            copies.append(
                pltpu.make_async_copy(source, out.at[:, pl.ds(x * width, width)], sem.at[2 * x + i])
            )
    for copy in copies:
        copy.start()
    for copy in copies:
        copy.wait()


def assemble(recv):
    total, width = recv.shape
    height = total // XS // 2
    shape = jax.ShapeDtypeStruct((height, XS * width), recv.dtype)
    return pl.pallas_call(
        assemble_kernel,
        in_specs=[pl.BlockSpec(memory_space=pl.ANY)],
        out_specs=[pl.BlockSpec(memory_space=pltpu.HBM)] * 2,
        out_shape=[shape] * 2,
        scratch_shapes=[pltpu.SemaphoreType.DMA((2 * XS,))],
        compiler_params=params(8),
        name="assemble",
    )(recv)


def exchange(pieces, axis):
    return lax.all_to_all(pieces, axis, split_axis=0, concat_axis=0, tiled=True)


def shift_x(array, steps):
    return lax.ppermute(array, "x", [(i, (i + steps) % XS) for i in range(XS)])


def body(
    features,
    own_features,
    neigh_index,
    neigh_count,
    degree,
    local_index,
    local_count,
    self_weight,
    neigh_weight,
    weight_two,
    weight_three,
    cotangent,
):
    groups = lax.axis_size(NODE)
    splits = lax.axis_size(FEAT)
    own_rows, width = own_features.shape
    slots = neigh_index.shape[2]
    per_x = own_rows * (groups // XS)

    place = lax.axis_index("x").reshape(1).astype(jnp.int32)
    payloads = make_payloads(place, neigh_index[0].T, neigh_count, features)
    arrived = [shift_x(payloads[s], s) for s in (2, 1, 3)]
    running = gather_sum(slots, per_x, jnp.float32, None, payloads[:1])
    running = gather_sum(slots, per_x, jnp.float32, running, arrived[1:])
    parts = gather_sum(slots, per_x, jnp.bfloat16, running, arrived[:1], staged=True)
    parts, own_late = lax.optimization_barrier((parts, own_features))
    own = [shift_x(own_late, s) for s in range(1, XS)]
    recv = exchange(parts.reshape(groups // XS, own_rows, width), "z")
    recv, *own = lax.optimization_barrier((recv, *own))
    mean_rows, pieces = first_layer(
        recv,
        degree[:, None].astype(jnp.float32),
        own_features,
        self_weight,
        neigh_weight,
        splits,
    )
    mean = [shift_x(mean_rows, s) for s in range(1, XS)]
    core = lax.axis_index("c").reshape(1).astype(jnp.int32)
    paired = pair_sum(core, lax.all_gather(pieces, "c", axis=0, tiled=False))
    paired, mean[0], mean[2] = lax.optimization_barrier((exchange(paired, "y"), mean[0], mean[2]))
    pre_copies = spread(paired, paired.shape[0])
    pre, mean[1] = lax.optimization_barrier((exchange(pre_copies, "y"), mean[1]))
    pre = lax.all_gather(pre, "c", axis=0, tiled=True)

    slot_ids = jnp.arange(local_index.shape[1], dtype=jnp.int32)
    live_slots = slot_ids[None, :] < local_count[:, None]
    slot_hits = (
        local_index[:, :, None] == jnp.arange(own_rows, dtype=jnp.int32)[None, None, :]
    ) & live_slots[:, :, None]
    adjacency = (
        jnp.sum(slot_hits.astype(jnp.float32), axis=1) + jnp.eye(own_rows, dtype=jnp.float32)
    ).astype(jnp.bfloat16)
    logits, grad_one = second_layer(
        pre, adjacency, weight_two, weight_three.T, cotangent.T
    )
    grad_part = gradient_part(place, [own_features] + own, [mean_rows] + mean, exchange(grad_one, "x"))
    quarter = grad_part.shape[1]
    grad_recv = exchange(grad_part.reshape(groups // XS, -1, quarter), "z")
    grads = exchange(spread(grad_recv, groups), NODE)
    grad_self, grad_neigh = assemble(grads.reshape(-1, quarter))
    return (grad_self, grad_neigh, logits.T)


def solution(mesh):
    nodes, feats = mesh.devices.shape
    fine = Mesh(mesh.devices.reshape(XS, nodes // XS, feats // 2, 2), ("x", "z", "y", "c"))
    in_specs = (
        P(NODE, FEAT),
        P(NODE, FEAT),
        P(NODE, None, None),
        P(NODE, None),
        P(NODE),
        P(NODE, None),
        P(NODE),
        P(FEAT, None),
        P(FEAT, None),
        P(),
        P(),
        P(NODE, None),
    )
    out_specs = (P(FEAT, None), P(FEAT, None), P(NODE, None))
    return jax.shard_map(body, mesh=fine, in_specs=in_specs, out_specs=out_specs, check_vma=False)
```

```python
import functools

import jax
import jax.numpy as jnp
from jax import lax
from jax.experimental import pallas as pl
from jax.experimental.pallas import tpu as pltpu
from jax.sharding import Mesh
from jax.sharding import PartitionSpec as P

XS = 4
ROW_BLOCK = 256
DEAD = 512.0
MIB = 1024 * 1024
NODE = ("x", "z")
FEAT = ("y", "c")


def silu_slope(value):
    gate = jax.nn.sigmoid(value)
    return gate + value * gate * (1.0 - gate)


def params(mib):
    return pltpu.CompilerParams(vmem_limit_bytes=mib * MIB)


def dot(a, b, dims=((1,), (0,))):
    return lax.dot_general(a, b, (dims, ((), ())), preferred_element_type=jnp.float32)


def payload_kernel(place_ref, index_hbm, count_hbm, table_hbm, *refs):
    outs = refs[:XS]
    index_ref, count_ref, table_ref, coded, sems = refs[XS:]
    nodes = table_hbm.shape[0]
    first = pltpu.make_async_copy(index_hbm, index_ref, sems.at[0])
    second = pltpu.make_async_copy(count_hbm, count_ref, sems.at[1])
    third = pltpu.make_async_copy(table_hbm, table_ref, sems.at[2 + 2 * XS])
    first.start()
    second.start()
    third.start()
    third.wait()
    copies = []
    for shift in range(XS):
        target = outs[shift].at[pl.ds(0, nodes), :]
        copies.append(pltpu.make_async_copy(table_ref, target, sems.at[2 + shift]))
        copies[shift].start()
    slots, total = index_ref.shape
    blocks = total // XS // ROW_BLOCK
    extra = coded.shape[1] - slots * blocks
    first.wait()
    second.wait()
    index = index_ref[...]
    slot = lax.broadcasted_iota(jnp.int32, (slots, total), 0)
    code = jnp.where(index < 256, index, 255 - index).astype(jnp.float32)
    code = jnp.where(slot < count_ref[...], code, DEAD)
    for x in range(XS):
        pieces = [
            code[:, (x * blocks + c) * ROW_BLOCK : (x * blocks + c + 1) * ROW_BLOCK]
            for c in range(blocks)
        ] + [jnp.full((extra, ROW_BLOCK), DEAD, jnp.float32)]
        coded[x] = jnp.concatenate(pieces, axis=0).astype(jnp.bfloat16)
    for shift in range(XS):
        source = coded.at[lax.rem(place_ref[0] + shift, XS)]
        target = outs[shift].at[pl.ds(nodes, coded.shape[1]), :]
        copies.append(pltpu.make_async_copy(source, target, sems.at[2 + XS + shift]))
        copies[XS + shift].start()
    for copy in copies:
        copy.wait()


def make_payloads(place, index, count, table):
    slots, total = index.shape
    nodes, width = table.shape
    used = slots * (total // XS // ROW_BLOCK)
    extra = -(-used // 16) * 16
    hbm = pl.BlockSpec(memory_space=pltpu.HBM)
    return pl.pallas_call(
        payload_kernel,
        in_specs=[pl.BlockSpec(memory_space=pltpu.SMEM), hbm, hbm, hbm],
        out_specs=[hbm] * XS,
        out_shape=[jax.ShapeDtypeStruct((nodes + extra, width), jnp.bfloat16)] * XS,
        scratch_shapes=[
            pltpu.VMEM(index.shape, index.dtype),
            pltpu.VMEM(count.shape, count.dtype),
            pltpu.VMEM(table.shape, table.dtype),
            pltpu.VMEM((XS, extra, ROW_BLOCK), jnp.bfloat16),
            pltpu.SemaphoreType.DMA((3 + 2 * XS,)),
        ],
        compiler_params=params(60),
        name="payloads",
    )(place, index, count, table)


def gather_kernel(slots, carried, staged, *refs):
    if staged:
        *refs, out_hbm, out_ref, sems = refs
        copies = []
    else:
        *refs, out_ref = refs
    payloads = refs[carried:]
    blocks = out_ref.shape[0] // ROW_BLOCK
    extra = -(-slots * blocks // 16) * 16
    nodes = payloads[0].shape[0] - extra
    lane = lax.broadcasted_iota(jnp.int32, (ROW_BLOCK, nodes), 1)
    node_code = jnp.where(lane < 256, lane, 255 - lane).astype(jnp.float32).astype(jnp.bfloat16)
    one = jnp.ones((), jnp.bfloat16)
    zero = jnp.zeros((), jnp.bfloat16)
    codes = [ref[nodes:, :].astype(jnp.float32).T.astype(jnp.bfloat16) for ref in payloads]
    for c in range(blocks):
        rows = slice(c * ROW_BLOCK, (c + 1) * ROW_BLOCK)
        total = refs[0][rows, :].astype(jnp.float32) if carried else None
        for ref, code in zip(payloads, codes):
            hits = None
            for k in range(slots):
                column = slots * c + k
                hit = jnp.where(code[:, column : column + 1] == node_code, one, zero)
                hits = hit if hits is None else hits + hit
            part = dot(hits, ref[0:nodes, :])
            total = part if total is None else total + part
        out_ref[rows, :] = total.astype(out_ref.dtype)
        if staged:
            block = pl.ds(c * ROW_BLOCK, ROW_BLOCK)
            copies.append(pltpu.make_async_copy(out_ref.at[block], out_hbm.at[block], sems.at[c]))
            copies[c].start()
    if staged:
        for copy in copies:
            copy.wait()


def gather_sum(slots, rows, dtype, carried, payloads, staged=False):
    width = payloads[0].shape[1]
    operands = ([carried] if carried is not None else []) + list(payloads)
    vmem = pl.BlockSpec(memory_space=pltpu.VMEM)
    return pl.pallas_call(
        functools.partial(gather_kernel, slots, int(carried is not None), staged),
        in_specs=[vmem] * len(operands),
        out_specs=pl.BlockSpec(memory_space=pl.ANY) if staged else vmem,
        out_shape=jax.ShapeDtypeStruct((rows, width), dtype),
        scratch_shapes=[
            pltpu.VMEM((rows, width), dtype),
            pltpu.SemaphoreType.DMA((rows // ROW_BLOCK,)),
        ]
        if staged
        else [],
        compiler_params=params(16),
        name="gather_sum",
    )(*operands)


def first_kernel(recv_ref, degree_ref, own_ref, self_ref, neigh_ref, mean_ref, out_ref):
    sums = recv_ref[0].astype(jnp.float32)
    for i in range(1, recv_ref.shape[0]):
        sums = sums + recv_ref[i].astype(jnp.float32)
    mean = (sums / degree_ref[...]).astype(jnp.bfloat16)
    mean_ref[...] = mean
    pre = (dot(own_ref[...], self_ref[...]) + dot(mean, neigh_ref[...])).astype(jnp.bfloat16)
    count, height, width = out_ref.shape
    halves = pre.shape[0] // height
    for i in range(count):
        t, h = i // halves, i % halves
        out_ref[i] = pre[h * height : (h + 1) * height, t * width : (t + 1) * width]


def first_layer(recv, degree, own, self_weight, neigh_weight, pieces):
    rows, width = own.shape
    hidden = self_weight.shape[1]
    vmem = pl.BlockSpec(memory_space=pltpu.VMEM)
    return pl.pallas_call(
        first_kernel,
        in_specs=[vmem] * 5,
        out_specs=[vmem] * 2,
        out_shape=[
            jax.ShapeDtypeStruct((rows, width), jnp.bfloat16),
            jax.ShapeDtypeStruct((pieces, rows // 2, 2 * hidden // pieces), jnp.bfloat16),
        ],
        compiler_params=params(16),
        name="first_layer",
    )(recv, degree, own, self_weight, neigh_weight)


def pair_kernel(core_ref, pieces_ref, out_ref):
    count = out_ref.shape[0]
    first = core_ref[0] * count
    for i in range(count):
        total = pieces_ref[0, first + i].astype(jnp.float32)
        for source in range(1, pieces_ref.shape[0]):
            total = total + pieces_ref[source, first + i].astype(jnp.float32)
        out_ref[i] = total.astype(jnp.bfloat16)


def pair_sum(core, pieces):
    cores, count, height, width = pieces.shape
    vmem = pl.BlockSpec(memory_space=pltpu.VMEM)
    return pl.pallas_call(
        pair_kernel,
        in_specs=[pl.BlockSpec(memory_space=pltpu.SMEM), vmem],
        out_specs=vmem,
        out_shape=jax.ShapeDtypeStruct((count // cores, height, width), jnp.bfloat16),
        compiler_params=params(8),
        name="pair_sum",
    )(core, pieces)


def second_kernel(
    pre_ref, adj_ref, two_ref, three_ref, cot_ref, logits_out, grad_ref, logits_ref, sem
):
    count, height, width = pre_ref.shape
    halves = adj_ref.shape[0] // height
    strips = [
        jnp.concatenate([pre_ref[t * halves + h] for h in range(halves)], axis=0)
        for t in range(count // halves)
    ]
    pre = jnp.concatenate(strips, axis=1).astype(jnp.float32)
    gate = jax.nn.sigmoid(pre)
    first_hidden = (pre * gate).astype(jnp.bfloat16)
    slope = (gate + pre * gate * (1.0 - gate)).astype(jnp.bfloat16).astype(jnp.float32)
    adjacency = adj_ref[...]
    inv = 1.0 / jnp.sum(adjacency.astype(jnp.float32), axis=1, keepdims=True)
    mixed = (dot(adjacency, first_hidden) * inv).astype(jnp.bfloat16)
    pre_two = dot(mixed, two_ref[...])
    gate_two = jax.nn.sigmoid(pre_two)
    second_hidden = (pre_two * gate_two).astype(jnp.bfloat16)
    across = ((1,), (1,))
    logits_ref[...] = dot(three_ref[...], second_hidden, across).astype(jnp.bfloat16)
    copy = pltpu.make_async_copy(logits_ref, logits_out, sem)
    copy.start()
    slope_two = gate_two + pre_two * gate_two * (1.0 - gate_two)
    back_two = dot(cot_ref[...], three_ref[...], ((0,), (0,)))
    grad_two = (back_two * slope_two).astype(jnp.bfloat16)
    grad_mixed = dot(grad_two, two_ref[...], across) * inv
    high = grad_mixed.astype(jnp.bfloat16)
    rest = grad_mixed - high.astype(jnp.float32)
    middle = rest.astype(jnp.bfloat16)
    low = (rest - middle.astype(jnp.float32)).astype(jnp.bfloat16)
    down = ((0,), (0,))
    grad_hidden = dot(adjacency, high, down) + (
        dot(adjacency, middle, down) + dot(adjacency, low, down)
    )
    grad_one = (grad_hidden * slope).astype(jnp.bfloat16)
    quarter = grad_ref.shape[2]
    for x in range(grad_ref.shape[0]):
        grad_ref[x] = grad_one[:, x * quarter : (x + 1) * quarter]
    copy.wait()


def second_layer(pre, adjacency, weight_two, weight_three, cotangent):
    rows = adjacency.shape[0]
    hidden = weight_two.shape[0]
    classes = weight_three.shape[0]
    vmem = pl.BlockSpec(memory_space=pltpu.VMEM)
    return pl.pallas_call(
        second_kernel,
        in_specs=[vmem] * 5,
        out_specs=[pl.BlockSpec(memory_space=pl.ANY), vmem],
        out_shape=[
            jax.ShapeDtypeStruct((classes, rows), jnp.bfloat16),
            jax.ShapeDtypeStruct((XS, rows, hidden // XS), jnp.bfloat16),
        ],
        scratch_shapes=[
            pltpu.VMEM((classes, rows), jnp.bfloat16),
            pltpu.SemaphoreType.DMA(()),
        ],
        compiler_params=params(24),
        name="second_layer",
    )(pre, adjacency, weight_two, weight_three, cotangent)


def gradient_kernel(place_ref, *refs):
    operands, grad_ref, out_ref = refs[:-2], refs[-2], refs[-1]
    width = operands[0].shape[1]
    for half in range(2):
        total = None
        for shift in range(XS):
            source = lax.rem(place_ref[0] + (XS - shift), XS)
            rows = operands[half * XS + shift][...]
            part = dot(rows, grad_ref[source], ((0,), (0,)))
            total = part if total is None else total + part
        out_ref[half * width : (half + 1) * width, :] = total.astype(jnp.bfloat16)


def gradient_part(place, own, mean, grad):
    vmem = pl.BlockSpec(memory_space=pltpu.VMEM)
    return pl.pallas_call(
        gradient_kernel,
        in_specs=[pl.BlockSpec(memory_space=pltpu.SMEM)] + [vmem] * (2 * XS + 1),
        out_specs=vmem,
        out_shape=jax.ShapeDtypeStruct((2 * own[0].shape[1], grad.shape[2]), jnp.bfloat16),
        compiler_params=params(16),
        name="gradient_part",
    )(place, *own, *mean, grad)


def spread_kernel(recv_ref, out_ref):
    sums = recv_ref[0].astype(jnp.float32)
    for i in range(1, recv_ref.shape[0]):
        sums = sums + recv_ref[i].astype(jnp.float32)
    piece = sums.astype(jnp.bfloat16)
    for i in range(out_ref.shape[0]):
        out_ref[i] = piece


def spread(recv, copies):
    vmem = pl.BlockSpec(memory_space=pltpu.VMEM)
    return pl.pallas_call(
        spread_kernel,
        in_specs=[vmem],
        out_specs=vmem,
        out_shape=jax.ShapeDtypeStruct((copies,) + recv.shape[1:], recv.dtype),
        compiler_params=params(8),
        name="sum_and_spread",
    )(recv)


def assemble_kernel(recv_hbm, self_hbm, neigh_hbm, sem):
    height, hidden = self_hbm.shape
    width = recv_hbm.shape[1]
    copies = []
    for x in range(hidden // width):
        for i, out in enumerate((self_hbm, neigh_hbm)):
            source = recv_hbm.at[pl.ds((2 * x + i) * height, height), :]
            copies.append(
                pltpu.make_async_copy(source, out.at[:, pl.ds(x * width, width)], sem.at[2 * x + i])
            )
    for copy in copies:
        copy.start()
    for copy in copies:
        copy.wait()


def assemble(recv):
    total, width = recv.shape
    height = total // XS // 2
    shape = jax.ShapeDtypeStruct((height, XS * width), recv.dtype)
    return pl.pallas_call(
        assemble_kernel,
        in_specs=[pl.BlockSpec(memory_space=pl.ANY)],
        out_specs=[pl.BlockSpec(memory_space=pltpu.HBM)] * 2,
        out_shape=[shape] * 2,
        scratch_shapes=[pltpu.SemaphoreType.DMA((2 * XS,))],
        compiler_params=params(8),
        name="assemble",
    )(recv)


def exchange(pieces, axis):
    return lax.all_to_all(pieces, axis, split_axis=0, concat_axis=0, tiled=True)


def shift_x(array, steps):
    return lax.ppermute(array, "x", [(i, (i + steps) % XS) for i in range(XS)])


def body(
    features,
    own_features,
    neigh_index,
    neigh_count,
    degree,
    local_index,
    local_count,
    self_weight,
    neigh_weight,
    weight_two,
    weight_three,
    cotangent,
):
    groups = lax.axis_size(NODE)
    splits = lax.axis_size(FEAT)
    own_rows, width = own_features.shape
    slots = neigh_index.shape[2]
    per_x = own_rows * (groups // XS)

    place = lax.axis_index("x").reshape(1).astype(jnp.int32)
    payloads = make_payloads(place, neigh_index[0].T, neigh_count, features)
    arrived = [shift_x(payloads[s], s) for s in (2, 1, 3)]
    running = gather_sum(slots, per_x, jnp.float32, None, payloads[:1])
    running = gather_sum(slots, per_x, jnp.float32, running, arrived[1:])
    parts = gather_sum(slots, per_x, jnp.bfloat16, running, arrived[:1], staged=True)
    parts, own_late = lax.optimization_barrier((parts, own_features))
    own = [shift_x(own_late, s) for s in range(1, XS)]
    recv = exchange(parts.reshape(groups // XS, own_rows, width), "z")
    recv, *own = lax.optimization_barrier((recv, *own))
    mean_rows, pieces = first_layer(
        recv,
        degree[:, None].astype(jnp.float32),
        own_features,
        self_weight,
        neigh_weight,
        splits,
    )
    mean = [shift_x(mean_rows, s) for s in range(1, XS)]
    core = lax.axis_index("c").reshape(1).astype(jnp.int32)
    paired = pair_sum(core, lax.all_gather(pieces, "c", axis=0, tiled=False))
    paired, mean[0] = lax.optimization_barrier((exchange(paired, "y"), mean[0]))
    pre_copies = spread(paired, paired.shape[0])
    pre = lax.all_gather(exchange(pre_copies, "y"), "c", axis=0, tiled=True)
    pre, mean[1], mean[2] = lax.optimization_barrier((pre, mean[1], mean[2]))

    slot_ids = jnp.arange(local_index.shape[1], dtype=jnp.int32)
    live_slots = slot_ids[None, :] < local_count[:, None]
    slot_hits = (
        local_index[:, :, None] == jnp.arange(own_rows, dtype=jnp.int32)[None, None, :]
    ) & live_slots[:, :, None]
    adjacency = (
        jnp.sum(slot_hits.astype(jnp.float32), axis=1) + jnp.eye(own_rows, dtype=jnp.float32)
    ).astype(jnp.bfloat16)
    logits, grad_one = second_layer(
        pre, adjacency, weight_two, weight_three.T, cotangent.T
    )
    grad_part = gradient_part(place, [own_features] + own, [mean_rows] + mean, exchange(grad_one, "x"))
    quarter = grad_part.shape[1]
    grad_recv = exchange(grad_part.reshape(groups // XS, -1, quarter), "z")
    grads = exchange(spread(grad_recv, groups), NODE)
    grad_self, grad_neigh = assemble(grads.reshape(-1, quarter))
    return (grad_self, grad_neigh, logits.T)


def solution(mesh):
    nodes, feats = mesh.devices.shape
    fine = Mesh(mesh.devices.reshape(XS, nodes // XS, feats // 2, 2), ("x", "z", "y", "c"))
    in_specs = (
        P(NODE, FEAT),
        P(NODE, FEAT),
        P(NODE, None, None),
        P(NODE, None),
        P(NODE),
        P(NODE, None),
        P(NODE),
        P(FEAT, None),
        P(FEAT, None),
        P(),
        P(),
        P(NODE, None),
    )
    out_specs = (P(FEAT, None), P(FEAT, None), P(NODE, None))
    return jax.shard_map(body, mesh=fine, in_specs=in_specs, out_specs=out_specs, check_vma=False)
```

```python
import functools

import jax
import jax.numpy as jnp
from jax import lax
from jax.experimental import pallas as pl
from jax.experimental.pallas import tpu as pltpu
from jax.sharding import Mesh
from jax.sharding import PartitionSpec as P

XS = 4
ROW_BLOCK = 256
DEAD = 512.0
MIB = 1024 * 1024
NODE = ("x", "z")
FEAT = ("y", "c")


def silu_slope(value):
    gate = jax.nn.sigmoid(value)
    return gate + value * gate * (1.0 - gate)


def params(mib):
    return pltpu.CompilerParams(vmem_limit_bytes=mib * MIB)


def dot(a, b, dims=((1,), (0,))):
    return lax.dot_general(a, b, (dims, ((), ())), preferred_element_type=jnp.float32)


def payload_kernel(place_ref, index_hbm, count_hbm, table_hbm, *refs):
    outs = refs[:XS]
    index_ref, count_ref, table_ref, coded, sems = refs[XS:]
    nodes = table_hbm.shape[0]
    first = pltpu.make_async_copy(index_hbm, index_ref, sems.at[0])
    second = pltpu.make_async_copy(count_hbm, count_ref, sems.at[1])
    third = pltpu.make_async_copy(table_hbm, table_ref, sems.at[2 + 2 * XS])
    first.start()
    second.start()
    third.start()
    third.wait()
    copies = []
    for shift in range(XS):
        target = outs[shift].at[pl.ds(0, nodes), :]
        copies.append(pltpu.make_async_copy(table_ref, target, sems.at[2 + shift]))
        copies[shift].start()
    slots, total = index_ref.shape
    blocks = total // XS // ROW_BLOCK
    extra = coded.shape[1] - slots * blocks
    first.wait()
    second.wait()
    index = index_ref[...]
    slot = lax.broadcasted_iota(jnp.int32, (slots, total), 0)
    code = jnp.where(index < 256, index, 255 - index).astype(jnp.float32)
    code = jnp.where(slot < count_ref[...], code, DEAD)
    for x in range(XS):
        pieces = [
            code[:, (x * blocks + c) * ROW_BLOCK : (x * blocks + c + 1) * ROW_BLOCK]
            for c in range(blocks)
        ] + [jnp.full((extra, ROW_BLOCK), DEAD, jnp.float32)]
        coded[x] = jnp.concatenate(pieces, axis=0).astype(jnp.bfloat16)
    for shift in range(XS):
        source = coded.at[lax.rem(place_ref[0] + shift, XS)]
        target = outs[shift].at[pl.ds(nodes, coded.shape[1]), :]
        copies.append(pltpu.make_async_copy(source, target, sems.at[2 + XS + shift]))
        copies[XS + shift].start()
    for copy in copies:
        copy.wait()


def make_payloads(place, index, count, table):
    slots, total = index.shape
    nodes, width = table.shape
    used = slots * (total // XS // ROW_BLOCK)
    extra = -(-used // 16) * 16
    hbm = pl.BlockSpec(memory_space=pltpu.HBM)
    return pl.pallas_call(
        payload_kernel,
        in_specs=[pl.BlockSpec(memory_space=pltpu.SMEM), hbm, hbm, hbm],
        out_specs=[hbm] * XS,
        out_shape=[jax.ShapeDtypeStruct((nodes + extra, width), jnp.bfloat16)] * XS,
        scratch_shapes=[
            pltpu.VMEM(index.shape, index.dtype),
            pltpu.VMEM(count.shape, count.dtype),
            pltpu.VMEM(table.shape, table.dtype),
            pltpu.VMEM((XS, extra, ROW_BLOCK), jnp.bfloat16),
            pltpu.SemaphoreType.DMA((3 + 2 * XS,)),
        ],
        compiler_params=params(60),
        name="payloads",
    )(place, index, count, table)


def gather_kernel(slots, carried, staged, *refs):
    if staged:
        *refs, out_hbm, out_ref, sems = refs
        copies = []
    else:
        *refs, out_ref = refs
    payloads = refs[carried:]
    blocks = out_ref.shape[0] // ROW_BLOCK
    extra = -(-slots * blocks // 16) * 16
    nodes = payloads[0].shape[0] - extra
    lane = lax.broadcasted_iota(jnp.int32, (ROW_BLOCK, nodes), 1)
    node_code = jnp.where(lane < 256, lane, 255 - lane).astype(jnp.float32).astype(jnp.bfloat16)
    one = jnp.ones((), jnp.bfloat16)
    zero = jnp.zeros((), jnp.bfloat16)
    codes = [ref[nodes:, :].astype(jnp.float32).T.astype(jnp.bfloat16) for ref in payloads]
    for c in range(blocks):
        rows = slice(c * ROW_BLOCK, (c + 1) * ROW_BLOCK)
        total = refs[0][rows, :].astype(jnp.float32) if carried else None
        for ref, code in zip(payloads, codes):
            hits = None
            for k in range(slots):
                column = slots * c + k
                hit = jnp.where(code[:, column : column + 1] == node_code, one, zero)
                hits = hit if hits is None else hits + hit
            part = dot(hits, ref[0:nodes, :])
            total = part if total is None else total + part
        out_ref[rows, :] = total.astype(out_ref.dtype)
        if staged:
            block = pl.ds(c * ROW_BLOCK, ROW_BLOCK)
            copies.append(pltpu.make_async_copy(out_ref.at[block], out_hbm.at[block], sems.at[c]))
            copies[c].start()
    if staged:
        for copy in copies:
            copy.wait()


def gather_sum(slots, rows, dtype, carried, payloads, staged=False):
    width = payloads[0].shape[1]
    operands = ([carried] if carried is not None else []) + list(payloads)
    vmem = pl.BlockSpec(memory_space=pltpu.VMEM)
    return pl.pallas_call(
        functools.partial(gather_kernel, slots, int(carried is not None), staged),
        in_specs=[vmem] * len(operands),
        out_specs=pl.BlockSpec(memory_space=pl.ANY) if staged else vmem,
        out_shape=jax.ShapeDtypeStruct((rows, width), dtype),
        scratch_shapes=[
            pltpu.VMEM((rows, width), dtype),
            pltpu.SemaphoreType.DMA((rows // ROW_BLOCK,)),
        ]
        if staged
        else [],
        compiler_params=params(16),
        name="gather_sum",
    )(*operands)


def first_kernel(recv_ref, degree_ref, own_ref, self_ref, neigh_ref, mean_ref, out_ref):
    sums = recv_ref[0].astype(jnp.float32)
    for i in range(1, recv_ref.shape[0]):
        sums = sums + recv_ref[i].astype(jnp.float32)
    mean = (sums / degree_ref[...]).astype(jnp.bfloat16)
    mean_ref[...] = mean
    pre = (dot(own_ref[...], self_ref[...]) + dot(mean, neigh_ref[...])).astype(jnp.bfloat16)
    count, height, width = out_ref.shape
    halves = pre.shape[0] // height
    for i in range(count):
        t, h = i // halves, i % halves
        out_ref[i] = pre[h * height : (h + 1) * height, t * width : (t + 1) * width]


def first_layer(recv, degree, own, self_weight, neigh_weight, pieces):
    rows, width = own.shape
    hidden = self_weight.shape[1]
    vmem = pl.BlockSpec(memory_space=pltpu.VMEM)
    return pl.pallas_call(
        first_kernel,
        in_specs=[vmem] * 5,
        out_specs=[vmem] * 2,
        out_shape=[
            jax.ShapeDtypeStruct((rows, width), jnp.bfloat16),
            jax.ShapeDtypeStruct((pieces, rows // 2, 2 * hidden // pieces), jnp.bfloat16),
        ],
        compiler_params=params(16),
        name="first_layer",
    )(recv, degree, own, self_weight, neigh_weight)


def pair_kernel(core_ref, pieces_ref, out_ref):
    count = out_ref.shape[0]
    first = core_ref[0] * count
    for i in range(count):
        total = pieces_ref[0, first + i].astype(jnp.float32)
        for source in range(1, pieces_ref.shape[0]):
            total = total + pieces_ref[source, first + i].astype(jnp.float32)
        out_ref[i] = total.astype(jnp.bfloat16)


def pair_sum(core, pieces):
    cores, count, height, width = pieces.shape
    vmem = pl.BlockSpec(memory_space=pltpu.VMEM)
    return pl.pallas_call(
        pair_kernel,
        in_specs=[pl.BlockSpec(memory_space=pltpu.SMEM), vmem],
        out_specs=vmem,
        out_shape=jax.ShapeDtypeStruct((count // cores, height, width), jnp.bfloat16),
        compiler_params=params(8),
        name="pair_sum",
    )(core, pieces)


def second_kernel(
    pre_ref, adj_ref, two_ref, three_ref, cot_ref, logits_ref, grad_ref
):
    count, height, width = pre_ref.shape
    halves = adj_ref.shape[0] // height
    strips = [
        jnp.concatenate([pre_ref[t * halves + h] for h in range(halves)], axis=0)
        for t in range(count // halves)
    ]
    pre = jnp.concatenate(strips, axis=1).astype(jnp.float32)
    gate = jax.nn.sigmoid(pre)
    first_hidden = (pre * gate).astype(jnp.bfloat16)
    slope = (gate + pre * gate * (1.0 - gate)).astype(jnp.bfloat16).astype(jnp.float32)
    adjacency = adj_ref[...]
    inv = 1.0 / jnp.sum(adjacency.astype(jnp.float32), axis=1, keepdims=True)
    mixed = (dot(adjacency, first_hidden) * inv).astype(jnp.bfloat16)
    pre_two = dot(mixed, two_ref[...])
    gate_two = jax.nn.sigmoid(pre_two)
    second_hidden = (pre_two * gate_two).astype(jnp.bfloat16)
    across = ((1,), (1,))
    logits_ref[...] = dot(three_ref[...], second_hidden, across).astype(jnp.bfloat16)
    slope_two = gate_two + pre_two * gate_two * (1.0 - gate_two)
    back_two = dot(cot_ref[...], three_ref[...], ((0,), (0,)))
    grad_two = (back_two * slope_two).astype(jnp.bfloat16)
    grad_mixed = dot(grad_two, two_ref[...], across) * inv
    high = grad_mixed.astype(jnp.bfloat16)
    rest = grad_mixed - high.astype(jnp.float32)
    middle = rest.astype(jnp.bfloat16)
    low = (rest - middle.astype(jnp.float32)).astype(jnp.bfloat16)
    down = ((0,), (0,))
    grad_hidden = dot(adjacency, high, down) + (
        dot(adjacency, middle, down) + dot(adjacency, low, down)
    )
    grad_one = (grad_hidden * slope).astype(jnp.bfloat16)
    quarter = grad_ref.shape[2]
    for x in range(grad_ref.shape[0]):
        grad_ref[x] = grad_one[:, x * quarter : (x + 1) * quarter]


def second_layer(pre, adjacency, weight_two, weight_three, cotangent):
    rows = adjacency.shape[0]
    hidden = weight_two.shape[0]
    classes = weight_three.shape[0]
    vmem = pl.BlockSpec(memory_space=pltpu.VMEM)
    return pl.pallas_call(
        second_kernel,
        in_specs=[vmem] * 5,
        out_specs=[vmem] * 2,
        out_shape=[
            jax.ShapeDtypeStruct((classes, rows), jnp.bfloat16),
            jax.ShapeDtypeStruct((XS, rows, hidden // XS), jnp.bfloat16),
        ],
        compiler_params=params(24),
        name="second_layer",
    )(pre, adjacency, weight_two, weight_three, cotangent)


def gradient_kernel(place_ref, *refs):
    operands, grad_ref, out_ref = refs[:-2], refs[-2], refs[-1]
    width = operands[0].shape[1]
    for half in range(2):
        total = None
        for shift in range(XS):
            source = lax.rem(place_ref[0] + (XS - shift), XS)
            rows = operands[half * XS + shift][...]
            part = dot(rows, grad_ref[source], ((0,), (0,)))
            total = part if total is None else total + part
        out_ref[half * width : (half + 1) * width, :] = total.astype(jnp.bfloat16)


def gradient_part(place, own, mean, grad):
    vmem = pl.BlockSpec(memory_space=pltpu.VMEM)
    return pl.pallas_call(
        gradient_kernel,
        in_specs=[pl.BlockSpec(memory_space=pltpu.SMEM)] + [vmem] * (2 * XS + 1),
        out_specs=vmem,
        out_shape=jax.ShapeDtypeStruct((2 * own[0].shape[1], grad.shape[2]), jnp.bfloat16),
        compiler_params=params(16),
        name="gradient_part",
    )(place, *own, *mean, grad)


def spread_kernel(recv_ref, out_ref):
    sums = recv_ref[0].astype(jnp.float32)
    for i in range(1, recv_ref.shape[0]):
        sums = sums + recv_ref[i].astype(jnp.float32)
    piece = sums.astype(jnp.bfloat16)
    for i in range(out_ref.shape[0]):
        out_ref[i] = piece


def spread(recv, copies):
    vmem = pl.BlockSpec(memory_space=pltpu.VMEM)
    return pl.pallas_call(
        spread_kernel,
        in_specs=[vmem],
        out_specs=vmem,
        out_shape=jax.ShapeDtypeStruct((copies,) + recv.shape[1:], recv.dtype),
        compiler_params=params(8),
        name="sum_and_spread",
    )(recv)


def assemble_kernel(recv_hbm, self_hbm, neigh_hbm, sem):
    height, hidden = self_hbm.shape
    width = recv_hbm.shape[1]
    copies = []
    for x in range(hidden // width):
        for i, out in enumerate((self_hbm, neigh_hbm)):
            source = recv_hbm.at[pl.ds((2 * x + i) * height, height), :]
            copies.append(
                pltpu.make_async_copy(source, out.at[:, pl.ds(x * width, width)], sem.at[2 * x + i])
            )
    for copy in copies:
        copy.start()
    for copy in copies:
        copy.wait()


def assemble(recv):
    total, width = recv.shape
    height = total // XS // 2
    shape = jax.ShapeDtypeStruct((height, XS * width), recv.dtype)
    return pl.pallas_call(
        assemble_kernel,
        in_specs=[pl.BlockSpec(memory_space=pl.ANY)],
        out_specs=[pl.BlockSpec(memory_space=pltpu.HBM)] * 2,
        out_shape=[shape] * 2,
        scratch_shapes=[pltpu.SemaphoreType.DMA((2 * XS,))],
        compiler_params=params(8),
        name="assemble",
    )(recv)


def exchange(pieces, axis):
    return lax.all_to_all(pieces, axis, split_axis=0, concat_axis=0, tiled=True)


def shift_x(array, steps):
    return lax.ppermute(array, "x", [(i, (i + steps) % XS) for i in range(XS)])


def body(
    features,
    own_features,
    neigh_index,
    neigh_count,
    degree,
    local_index,
    local_count,
    self_weight,
    neigh_weight,
    weight_two,
    weight_three,
    cotangent,
):
    groups = lax.axis_size(NODE)
    splits = lax.axis_size(FEAT)
    own_rows, width = own_features.shape
    slots = neigh_index.shape[2]
    per_x = own_rows * (groups // XS)

    place = lax.axis_index("x").reshape(1).astype(jnp.int32)
    payloads = make_payloads(place, neigh_index[0].T, neigh_count, features)
    arrived = [shift_x(payloads[s], s) for s in (2, 1, 3)]
    running = gather_sum(slots, per_x, jnp.float32, None, payloads[:1])
    running = gather_sum(slots, per_x, jnp.float32, running, arrived[1:])
    parts = gather_sum(slots, per_x, jnp.bfloat16, running, arrived[:1], staged=True)
    parts, own_late = lax.optimization_barrier((parts, own_features))
    own = [shift_x(own_late, s) for s in range(1, XS)]
    recv = exchange(parts.reshape(groups // XS, own_rows, width), "z")
    recv, *own = lax.optimization_barrier((recv, *own))
    mean_rows, pieces = first_layer(
        recv,
        degree[:, None].astype(jnp.float32),
        own_features,
        self_weight,
        neigh_weight,
        splits,
    )
    mean = [shift_x(mean_rows, s) for s in range(1, XS)]
    core = lax.axis_index("c").reshape(1).astype(jnp.int32)
    paired = pair_sum(core, lax.all_gather(pieces, "c", axis=0, tiled=False))
    paired, mean[0] = lax.optimization_barrier((exchange(paired, "y"), mean[0]))
    pre_copies = spread(paired, paired.shape[0])
    pre = lax.all_gather(exchange(pre_copies, "y"), "c", axis=0, tiled=True)
    pre, mean[1], mean[2] = lax.optimization_barrier((pre, mean[1], mean[2]))

    slot_ids = jnp.arange(local_index.shape[1], dtype=jnp.int32)
    live_slots = slot_ids[None, :] < local_count[:, None]
    slot_hits = (
        local_index[:, :, None] == jnp.arange(own_rows, dtype=jnp.int32)[None, None, :]
    ) & live_slots[:, :, None]
    adjacency = (
        jnp.sum(slot_hits.astype(jnp.float32), axis=1) + jnp.eye(own_rows, dtype=jnp.float32)
    ).astype(jnp.bfloat16)
    logits, grad_one = second_layer(
        pre, adjacency, weight_two, weight_three.T, cotangent.T
    )
    grad_part = gradient_part(place, [own_features] + own, [mean_rows] + mean, exchange(grad_one, "x"))
    quarter = grad_part.shape[1]
    grad_recv = exchange(grad_part.reshape(groups // XS, -1, quarter), "z")
    grads = exchange(spread(grad_recv, groups), NODE)
    grad_self, grad_neigh = assemble(grads.reshape(-1, quarter))
    return (grad_self, grad_neigh, logits.T)


def solution(mesh):
    nodes, feats = mesh.devices.shape
    fine = Mesh(mesh.devices.reshape(XS, nodes // XS, feats // 2, 2), ("x", "z", "y", "c"))
    in_specs = (
        P(NODE, FEAT),
        P(NODE, FEAT),
        P(NODE, None, None),
        P(NODE, None),
        P(NODE),
        P(NODE, None),
        P(NODE),
        P(FEAT, None),
        P(FEAT, None),
        P(),
        P(),
        P(NODE, None),
    )
    out_specs = (P(FEAT, None), P(FEAT, None), P(NODE, None))
    return jax.shard_map(body, mesh=fine, in_specs=in_specs, out_specs=out_specs, check_vma=False)
```

```python
import functools

import jax
import jax.numpy as jnp
from jax import lax
from jax.experimental import pallas as pl
from jax.experimental.pallas import tpu as pltpu
from jax.sharding import Mesh
from jax.sharding import PartitionSpec as P

XS = 4
ROW_BLOCK = 256
DEAD = 512.0
MIB = 1024 * 1024
NODE = ("x", "z")
FEAT = ("y", "c")


def silu_slope(value):
    gate = jax.nn.sigmoid(value)
    return gate + value * gate * (1.0 - gate)


def params(mib):
    return pltpu.CompilerParams(vmem_limit_bytes=mib * MIB)


def dot(a, b, dims=((1,), (0,))):
    return lax.dot_general(a, b, (dims, ((), ())), preferred_element_type=jnp.float32)


def payload_kernel(place_ref, index_hbm, count_hbm, table_hbm, *refs):
    outs = refs[:XS]
    index_ref, count_ref, table_ref, coded, sems = refs[XS:]
    nodes = table_hbm.shape[0]
    first = pltpu.make_async_copy(index_hbm, index_ref, sems.at[0])
    second = pltpu.make_async_copy(count_hbm, count_ref, sems.at[1])
    third = pltpu.make_async_copy(table_hbm, table_ref, sems.at[2 + 2 * XS])
    first.start()
    second.start()
    third.start()
    third.wait()
    copies = []
    for shift in range(XS):
        target = outs[shift].at[pl.ds(0, nodes), :]
        copies.append(pltpu.make_async_copy(table_ref, target, sems.at[2 + shift]))
        copies[shift].start()
    slots, total = index_ref.shape
    blocks = total // XS // ROW_BLOCK
    extra = coded.shape[1] - slots * blocks
    first.wait()
    second.wait()
    index = index_ref[...]
    slot = lax.broadcasted_iota(jnp.int32, (slots, total), 0)
    code = jnp.where(index < 256, index, 255 - index).astype(jnp.float32)
    code = jnp.where(slot < count_ref[...], code, DEAD)
    for x in range(XS):
        pieces = [
            code[:, (x * blocks + c) * ROW_BLOCK : (x * blocks + c + 1) * ROW_BLOCK]
            for c in range(blocks)
        ] + [jnp.full((extra, ROW_BLOCK), DEAD, jnp.float32)]
        coded[x] = jnp.concatenate(pieces, axis=0).astype(jnp.bfloat16)
    for shift in range(XS):
        source = coded.at[lax.rem(place_ref[0] + shift, XS)]
        target = outs[shift].at[pl.ds(nodes, coded.shape[1]), :]
        copies.append(pltpu.make_async_copy(source, target, sems.at[2 + XS + shift]))
        copies[XS + shift].start()
    for copy in copies:
        copy.wait()


def make_payloads(place, index, count, table):
    slots, total = index.shape
    nodes, width = table.shape
    used = slots * (total // XS // ROW_BLOCK)
    extra = -(-used // 16) * 16
    hbm = pl.BlockSpec(memory_space=pltpu.HBM)
    return pl.pallas_call(
        payload_kernel,
        in_specs=[pl.BlockSpec(memory_space=pltpu.SMEM), hbm, hbm, hbm],
        out_specs=[hbm] * XS,
        out_shape=[jax.ShapeDtypeStruct((nodes + extra, width), jnp.bfloat16)] * XS,
        scratch_shapes=[
            pltpu.VMEM(index.shape, index.dtype),
            pltpu.VMEM(count.shape, count.dtype),
            pltpu.VMEM(table.shape, table.dtype),
            pltpu.VMEM((XS, extra, ROW_BLOCK), jnp.bfloat16),
            pltpu.SemaphoreType.DMA((3 + 2 * XS,)),
        ],
        compiler_params=params(60),
        name="payloads",
    )(place, index, count, table)


def gather_kernel(slots, carried, staged, *refs):
    if staged:
        *refs, out_hbm, out_ref, sems = refs
        copies = []
    else:
        *refs, out_ref = refs
    payloads = refs[carried:]
    blocks = out_ref.shape[0] // ROW_BLOCK
    extra = -(-slots * blocks // 16) * 16
    nodes = payloads[0].shape[0] - extra
    lane = lax.broadcasted_iota(jnp.int32, (ROW_BLOCK, nodes), 1)
    node_code = jnp.where(lane < 256, lane, 255 - lane).astype(jnp.float32).astype(jnp.bfloat16)
    one = jnp.ones((), jnp.bfloat16)
    zero = jnp.zeros((), jnp.bfloat16)
    codes = [ref[nodes:, :].astype(jnp.float32).T.astype(jnp.bfloat16) for ref in payloads]
    for c in range(blocks):
        rows = slice(c * ROW_BLOCK, (c + 1) * ROW_BLOCK)
        total = refs[0][rows, :].astype(jnp.float32) if carried else None
        for ref, code in zip(payloads, codes):
            hits = None
            for k in range(slots):
                column = slots * c + k
                hit = jnp.where(code[:, column : column + 1] == node_code, one, zero)
                hits = hit if hits is None else hits + hit
            part = dot(hits, ref[0:nodes, :])
            total = part if total is None else total + part
        out_ref[rows, :] = total.astype(out_ref.dtype)
        if staged:
            block = pl.ds(c * ROW_BLOCK, ROW_BLOCK)
            copies.append(pltpu.make_async_copy(out_ref.at[block], out_hbm.at[block], sems.at[c]))
            copies[c].start()
    if staged:
        for copy in copies:
            copy.wait()


def gather_sum(slots, rows, dtype, carried, payloads, staged=False):
    width = payloads[0].shape[1]
    operands = ([carried] if carried is not None else []) + list(payloads)
    vmem = pl.BlockSpec(memory_space=pltpu.VMEM)
    return pl.pallas_call(
        functools.partial(gather_kernel, slots, int(carried is not None), staged),
        in_specs=[vmem] * len(operands),
        out_specs=pl.BlockSpec(memory_space=pl.ANY) if staged else vmem,
        out_shape=jax.ShapeDtypeStruct((rows, width), dtype),
        scratch_shapes=[
            pltpu.VMEM((rows, width), dtype),
            pltpu.SemaphoreType.DMA((rows // ROW_BLOCK,)),
        ]
        if staged
        else [],
        compiler_params=params(16),
        name="gather_sum",
    )(*operands)


def first_kernel(recv_ref, degree_ref, own_ref, self_ref, neigh_ref, mean_ref, out_ref):
    sums = recv_ref[0].astype(jnp.float32)
    for i in range(1, recv_ref.shape[0]):
        sums = sums + recv_ref[i].astype(jnp.float32)
    mean = (sums / degree_ref[...]).astype(jnp.bfloat16)
    mean_ref[...] = mean
    pre = (dot(own_ref[...], self_ref[...]) + dot(mean, neigh_ref[...])).astype(jnp.bfloat16)
    count, height, width = out_ref.shape
    halves = pre.shape[0] // height
    for i in range(count):
        t, h = i // halves, i % halves
        out_ref[i] = pre[h * height : (h + 1) * height, t * width : (t + 1) * width]


def first_layer(recv, degree, own, self_weight, neigh_weight, pieces):
    rows, width = own.shape
    hidden = self_weight.shape[1]
    vmem = pl.BlockSpec(memory_space=pltpu.VMEM)
    return pl.pallas_call(
        first_kernel,
        in_specs=[vmem] * 5,
        out_specs=[vmem] * 2,
        out_shape=[
            jax.ShapeDtypeStruct((rows, width), jnp.bfloat16),
            jax.ShapeDtypeStruct((pieces, rows // 2, 2 * hidden // pieces), jnp.bfloat16),
        ],
        compiler_params=params(16),
        name="first_layer",
    )(recv, degree, own, self_weight, neigh_weight)


def pair_kernel(core_ref, pieces_ref, out_ref):
    count = out_ref.shape[0]
    first = core_ref[0] * count
    for i in range(count):
        total = pieces_ref[0, first + i].astype(jnp.float32)
        for source in range(1, pieces_ref.shape[0]):
            total = total + pieces_ref[source, first + i].astype(jnp.float32)
        out_ref[i] = total.astype(jnp.bfloat16)


def pair_sum(core, pieces):
    cores, count, height, width = pieces.shape
    vmem = pl.BlockSpec(memory_space=pltpu.VMEM)
    return pl.pallas_call(
        pair_kernel,
        in_specs=[pl.BlockSpec(memory_space=pltpu.SMEM), vmem],
        out_specs=vmem,
        out_shape=jax.ShapeDtypeStruct((count // cores, height, width), jnp.bfloat16),
        compiler_params=params(8),
        name="pair_sum",
    )(core, pieces)


def second_kernel(
    pre_ref, adj_ref, two_ref, three_ref, cot_ref, logits_ref, grad_ref
):
    count, height, width = pre_ref.shape
    halves = adj_ref.shape[0] // height
    strips = [
        jnp.concatenate([pre_ref[t * halves + h] for h in range(halves)], axis=0)
        for t in range(count // halves)
    ]
    pre = jnp.concatenate(strips, axis=1).astype(jnp.float32)
    gate = jax.nn.sigmoid(pre)
    first_hidden = (pre * gate).astype(jnp.bfloat16)
    slope = (gate + pre * gate * (1.0 - gate)).astype(jnp.bfloat16).astype(jnp.float32)
    adjacency = adj_ref[...]
    inv = 1.0 / jnp.sum(adjacency.astype(jnp.float32), axis=1, keepdims=True)
    mixed = (dot(adjacency, first_hidden) * inv).astype(jnp.bfloat16)
    pre_two = dot(mixed, two_ref[...])
    gate_two = jax.nn.sigmoid(pre_two)
    second_hidden = (pre_two * gate_two).astype(jnp.bfloat16)
    across = ((1,), (1,))
    logits_ref[...] = dot(three_ref[...], second_hidden, across).astype(jnp.bfloat16)
    slope_two = gate_two + pre_two * gate_two * (1.0 - gate_two)
    back_two = dot(cot_ref[...], three_ref[...], ((0,), (0,)))
    grad_two = (back_two * slope_two).astype(jnp.bfloat16)
    grad_mixed = dot(grad_two, two_ref[...], across) * inv
    high = grad_mixed.astype(jnp.bfloat16)
    rest = grad_mixed - high.astype(jnp.float32)
    middle = rest.astype(jnp.bfloat16)
    low = (rest - middle.astype(jnp.float32)).astype(jnp.bfloat16)
    down = ((0,), (0,))
    grad_hidden = dot(adjacency, high, down) + (
        dot(adjacency, middle, down) + dot(adjacency, low, down)
    )
    grad_one = (grad_hidden * slope).astype(jnp.bfloat16)
    quarter = grad_ref.shape[2]
    for x in range(grad_ref.shape[0]):
        grad_ref[x] = grad_one[:, x * quarter : (x + 1) * quarter]


def second_layer(pre, adjacency, weight_two, weight_three, cotangent):
    rows = adjacency.shape[0]
    hidden = weight_two.shape[0]
    classes = weight_three.shape[0]
    vmem = pl.BlockSpec(memory_space=pltpu.VMEM)
    return pl.pallas_call(
        second_kernel,
        in_specs=[vmem] * 5,
        out_specs=[vmem] * 2,
        out_shape=[
            jax.ShapeDtypeStruct((classes, rows), jnp.bfloat16),
            jax.ShapeDtypeStruct((XS, rows, hidden // XS), jnp.bfloat16),
        ],
        compiler_params=params(24),
        name="second_layer",
    )(pre, adjacency, weight_two, weight_three, cotangent)


def gradient_kernel(place_ref, *refs):
    operands, grad_ref, out_ref = refs[:-2], refs[-2], refs[-1]
    width = operands[0].shape[1]
    for half in range(2):
        total = None
        for shift in range(XS):
            source = lax.rem(place_ref[0] + (XS - shift), XS)
            rows = operands[half * XS + shift][...]
            part = dot(rows, grad_ref[source], ((0,), (0,)))
            total = part if total is None else total + part
        out_ref[half * width : (half + 1) * width, :] = total.astype(jnp.bfloat16)


def gradient_part(place, own, mean, grad):
    vmem = pl.BlockSpec(memory_space=pltpu.VMEM)
    return pl.pallas_call(
        gradient_kernel,
        in_specs=[pl.BlockSpec(memory_space=pltpu.SMEM)] + [vmem] * (2 * XS + 1),
        out_specs=vmem,
        out_shape=jax.ShapeDtypeStruct((2 * own[0].shape[1], grad.shape[2]), jnp.bfloat16),
        compiler_params=params(16),
        name="gradient_part",
    )(place, *own, *mean, grad)


def spread_kernel(recv_ref, out_ref):
    sums = recv_ref[0].astype(jnp.float32)
    for i in range(1, recv_ref.shape[0]):
        sums = sums + recv_ref[i].astype(jnp.float32)
    piece = sums.astype(jnp.bfloat16)
    for i in range(out_ref.shape[0]):
        out_ref[i] = piece


def spread(recv, copies):
    vmem = pl.BlockSpec(memory_space=pltpu.VMEM)
    return pl.pallas_call(
        spread_kernel,
        in_specs=[vmem],
        out_specs=vmem,
        out_shape=jax.ShapeDtypeStruct((copies,) + recv.shape[1:], recv.dtype),
        compiler_params=params(8),
        name="sum_and_spread",
    )(recv)


def assemble_kernel(recv_hbm, self_hbm, neigh_hbm, sem):
    height, hidden = self_hbm.shape
    width = recv_hbm.shape[1]
    copies = []
    for x in range(hidden // width):
        for i, out in enumerate((self_hbm, neigh_hbm)):
            source = recv_hbm.at[pl.ds((2 * x + i) * height, height), :]
            copies.append(
                pltpu.make_async_copy(source, out.at[:, pl.ds(x * width, width)], sem.at[2 * x + i])
            )
    for copy in copies:
        copy.start()
    for copy in copies:
        copy.wait()


def assemble(recv):
    total, width = recv.shape
    height = total // XS // 2
    shape = jax.ShapeDtypeStruct((height, XS * width), recv.dtype)
    return pl.pallas_call(
        assemble_kernel,
        in_specs=[pl.BlockSpec(memory_space=pl.ANY)],
        out_specs=[pl.BlockSpec(memory_space=pltpu.HBM)] * 2,
        out_shape=[shape] * 2,
        scratch_shapes=[pltpu.SemaphoreType.DMA((2 * XS,))],
        compiler_params=params(8),
        name="assemble",
    )(recv)


def exchange(pieces, axis):
    return lax.all_to_all(pieces, axis, split_axis=0, concat_axis=0, tiled=True)


def shift_x(array, steps):
    return lax.ppermute(array, "x", [(i, (i + steps) % XS) for i in range(XS)])


def body(
    features,
    own_features,
    neigh_index,
    neigh_count,
    degree,
    local_index,
    local_count,
    self_weight,
    neigh_weight,
    weight_two,
    weight_three,
    cotangent,
):
    groups = lax.axis_size(NODE)
    splits = lax.axis_size(FEAT)
    own_rows, width = own_features.shape
    slots = neigh_index.shape[2]
    per_x = own_rows * (groups // XS)

    place = lax.axis_index("x").reshape(1).astype(jnp.int32)
    payloads = make_payloads(place, neigh_index[0].T, neigh_count, features)
    arrived = [shift_x(payloads[s], s) for s in (2, 1, 3)]
    running = gather_sum(slots, per_x, jnp.float32, None, payloads[:1])
    running = gather_sum(slots, per_x, jnp.float32, running, arrived[1:])
    parts = gather_sum(slots, per_x, jnp.bfloat16, running, arrived[:1], staged=True)
    parts, own_late = lax.optimization_barrier((parts, own_features))
    own = [shift_x(own_late, s) for s in range(1, XS)]
    recv = exchange(parts.reshape(groups // XS, own_rows, width), "z")
    recv, *own = lax.optimization_barrier((recv, *own))
    mean_rows, pieces = first_layer(
        recv,
        degree[:, None].astype(jnp.float32),
        own_features,
        self_weight,
        neigh_weight,
        splits,
    )
    mean = [shift_x(mean_rows, s) for s in range(1, XS)]
    core = lax.axis_index("c").reshape(1).astype(jnp.int32)
    paired = pair_sum(core, lax.all_gather(pieces, "c", axis=0, tiled=False))
    paired, mean[0] = lax.optimization_barrier((exchange(paired, "y"), mean[0]))
    pre_copies = spread(paired, paired.shape[0])
    pre = lax.all_gather(exchange(pre_copies, "y"), "c", axis=0, tiled=True)
    pre, mean[1], mean[2] = lax.optimization_barrier((pre, mean[1], mean[2]))

    slot_ids = jnp.arange(local_index.shape[1], dtype=jnp.int32)
    live_slots = slot_ids[None, :] < local_count[:, None]
    slot_hits = (
        local_index[:, :, None] == jnp.arange(own_rows, dtype=jnp.int32)[None, None, :]
    ) & live_slots[:, :, None]
    adjacency = (
        jnp.sum(slot_hits.astype(jnp.float32), axis=1) + jnp.eye(own_rows, dtype=jnp.float32)
    ).astype(jnp.bfloat16)
    logits, grad_one = second_layer(
        pre, adjacency, weight_two, weight_three.T, cotangent.T
    )
    grad_part = gradient_part(place, [own_features] + own, [mean_rows] + mean, exchange(grad_one, "x"))
    quarter = grad_part.shape[1]
    grad_recv = exchange(grad_part.reshape(groups // XS, -1, quarter), "z")
    part = exchange(spread(grad_recv, groups // XS), "z")
    grads = exchange(spread(part.reshape(1, -1, quarter), XS), "x")
    grad_self, grad_neigh = assemble(grads.reshape(-1, quarter))
    return (grad_self, grad_neigh, logits.T)


def solution(mesh):
    nodes, feats = mesh.devices.shape
    fine = Mesh(mesh.devices.reshape(XS, nodes // XS, feats // 2, 2), ("x", "z", "y", "c"))
    in_specs = (
        P(NODE, FEAT),
        P(NODE, FEAT),
        P(NODE, None, None),
        P(NODE, None),
        P(NODE),
        P(NODE, None),
        P(NODE),
        P(FEAT, None),
        P(FEAT, None),
        P(),
        P(),
        P(NODE, None),
    )
    out_specs = (P(FEAT, None), P(FEAT, None), P(NODE, None))
    return jax.shard_map(body, mesh=fine, in_specs=in_specs, out_specs=out_specs, check_vma=False)
```

```python
import functools

import jax
import jax.numpy as jnp
from jax import lax
from jax.experimental import pallas as pl
from jax.experimental.pallas import tpu as pltpu
from jax.sharding import Mesh
from jax.sharding import PartitionSpec as P

XS = 4
ROW_BLOCK = 256
DEAD = 512.0
MIB = 1024 * 1024
NODE = ("x", "z")
FEAT = ("y", "c")


def silu_slope(value):
    gate = jax.nn.sigmoid(value)
    return gate + value * gate * (1.0 - gate)


def params(mib):
    return pltpu.CompilerParams(vmem_limit_bytes=mib * MIB)


def dot(a, b, dims=((1,), (0,))):
    return lax.dot_general(a, b, (dims, ((), ())), preferred_element_type=jnp.float32)


def payload_kernel(place_ref, index_hbm, count_hbm, table_hbm, *refs):
    outs = refs[:XS]
    index_ref, count_ref, table_ref, coded, sems = refs[XS:]
    nodes = table_hbm.shape[0]
    first = pltpu.make_async_copy(index_hbm, index_ref, sems.at[0])
    second = pltpu.make_async_copy(count_hbm, count_ref, sems.at[1])
    third = pltpu.make_async_copy(table_hbm, table_ref, sems.at[2 + 2 * XS])
    first.start()
    second.start()
    third.start()
    third.wait()
    copies = []
    for shift in range(XS):
        target = outs[shift].at[pl.ds(0, nodes), :]
        copies.append(pltpu.make_async_copy(table_ref, target, sems.at[2 + shift]))
        copies[shift].start()
    slots, total = index_ref.shape
    blocks = total // XS // ROW_BLOCK
    extra = coded.shape[1] - slots * blocks
    first.wait()
    second.wait()
    index = index_ref[...]
    slot = lax.broadcasted_iota(jnp.int32, (slots, total), 0)
    code = jnp.where(index < 256, index, 255 - index).astype(jnp.float32)
    code = jnp.where(slot < count_ref[...], code, DEAD)
    for x in range(XS):
        pieces = [
            code[:, (x * blocks + c) * ROW_BLOCK : (x * blocks + c + 1) * ROW_BLOCK]
            for c in range(blocks)
        ] + [jnp.full((extra, ROW_BLOCK), DEAD, jnp.float32)]
        coded[x] = jnp.concatenate(pieces, axis=0).astype(jnp.bfloat16)
    for shift in range(XS):
        source = coded.at[lax.rem(place_ref[0] + shift, XS)]
        target = outs[shift].at[pl.ds(nodes, coded.shape[1]), :]
        copies.append(pltpu.make_async_copy(source, target, sems.at[2 + XS + shift]))
        copies[XS + shift].start()
    for copy in copies:
        copy.wait()


def make_payloads(place, index, count, table):
    slots, total = index.shape
    nodes, width = table.shape
    used = slots * (total // XS // ROW_BLOCK)
    extra = -(-used // 16) * 16
    hbm = pl.BlockSpec(memory_space=pltpu.HBM)
    return pl.pallas_call(
        payload_kernel,
        in_specs=[pl.BlockSpec(memory_space=pltpu.SMEM), hbm, hbm, hbm],
        out_specs=[hbm] * XS,
        out_shape=[jax.ShapeDtypeStruct((nodes + extra, width), jnp.bfloat16)] * XS,
        scratch_shapes=[
            pltpu.VMEM(index.shape, index.dtype),
            pltpu.VMEM(count.shape, count.dtype),
            pltpu.VMEM(table.shape, table.dtype),
            pltpu.VMEM((XS, extra, ROW_BLOCK), jnp.bfloat16),
            pltpu.SemaphoreType.DMA((3 + 2 * XS,)),
        ],
        compiler_params=params(60),
        name="payloads",
    )(place, index, count, table)


def gather_kernel(slots, carried, staged, *refs):
    if staged:
        *refs, out_hbm, out_ref, sems = refs
        copies = []
    else:
        *refs, out_ref = refs
    payloads = refs[carried:]
    blocks = out_ref.shape[0] // ROW_BLOCK
    extra = -(-slots * blocks // 16) * 16
    nodes = payloads[0].shape[0] - extra
    lane = lax.broadcasted_iota(jnp.int32, (ROW_BLOCK, nodes), 1)
    node_code = jnp.where(lane < 256, lane, 255 - lane).astype(jnp.float32).astype(jnp.bfloat16)
    one = jnp.ones((), jnp.bfloat16)
    zero = jnp.zeros((), jnp.bfloat16)
    codes = [ref[nodes:, :].astype(jnp.float32).T.astype(jnp.bfloat16) for ref in payloads]
    for c in range(blocks):
        rows = slice(c * ROW_BLOCK, (c + 1) * ROW_BLOCK)
        total = refs[0][rows, :].astype(jnp.float32) if carried else None
        for ref, code in zip(payloads, codes):
            hits = None
            for k in range(slots):
                column = slots * c + k
                hit = jnp.where(code[:, column : column + 1] == node_code, one, zero)
                hits = hit if hits is None else hits + hit
            part = dot(hits, ref[0:nodes, :])
            total = part if total is None else total + part
        out_ref[rows, :] = total.astype(out_ref.dtype)
        if staged:
            block = pl.ds(c * ROW_BLOCK, ROW_BLOCK)
            copies.append(pltpu.make_async_copy(out_ref.at[block], out_hbm.at[block], sems.at[c]))
            copies[c].start()
    if staged:
        for copy in copies:
            copy.wait()


def gather_sum(slots, rows, dtype, carried, payloads, staged=False):
    width = payloads[0].shape[1]
    operands = ([carried] if carried is not None else []) + list(payloads)
    vmem = pl.BlockSpec(memory_space=pltpu.VMEM)
    return pl.pallas_call(
        functools.partial(gather_kernel, slots, int(carried is not None), staged),
        in_specs=[vmem] * len(operands),
        out_specs=pl.BlockSpec(memory_space=pl.ANY) if staged else vmem,
        out_shape=jax.ShapeDtypeStruct((rows, width), dtype),
        scratch_shapes=[
            pltpu.VMEM((rows, width), dtype),
            pltpu.SemaphoreType.DMA((rows // ROW_BLOCK,)),
        ]
        if staged
        else [],
        compiler_params=params(16),
        name="gather_sum",
    )(*operands)


def first_kernel(recv_ref, degree_ref, own_ref, self_ref, neigh_ref, mean_ref, out_ref):
    sums = recv_ref[0].astype(jnp.float32)
    for i in range(1, recv_ref.shape[0]):
        sums = sums + recv_ref[i].astype(jnp.float32)
    mean = (sums / degree_ref[...]).astype(jnp.bfloat16)
    mean_ref[...] = mean
    pre = (dot(own_ref[...], self_ref[...]) + dot(mean, neigh_ref[...])).astype(jnp.bfloat16)
    count, height, width = out_ref.shape
    halves = pre.shape[0] // height
    for i in range(count):
        t, h = i // halves, i % halves
        out_ref[i] = pre[h * height : (h + 1) * height, t * width : (t + 1) * width]


def first_layer(recv, degree, own, self_weight, neigh_weight, pieces):
    rows, width = own.shape
    hidden = self_weight.shape[1]
    vmem = pl.BlockSpec(memory_space=pltpu.VMEM)
    return pl.pallas_call(
        first_kernel,
        in_specs=[vmem] * 5,
        out_specs=[vmem] * 2,
        out_shape=[
            jax.ShapeDtypeStruct((rows, width), jnp.bfloat16),
            jax.ShapeDtypeStruct((pieces, rows // 2, 2 * hidden // pieces), jnp.bfloat16),
        ],
        compiler_params=params(16),
        name="first_layer",
    )(recv, degree, own, self_weight, neigh_weight)


def pair_kernel(core_ref, pieces_ref, out_ref):
    count = out_ref.shape[0]
    first = core_ref[0] * count
    for i in range(count):
        total = pieces_ref[0, first + i].astype(jnp.float32)
        for source in range(1, pieces_ref.shape[0]):
            total = total + pieces_ref[source, first + i].astype(jnp.float32)
        out_ref[i] = total.astype(jnp.bfloat16)


def pair_sum(core, pieces):
    cores, count, height, width = pieces.shape
    vmem = pl.BlockSpec(memory_space=pltpu.VMEM)
    return pl.pallas_call(
        pair_kernel,
        in_specs=[pl.BlockSpec(memory_space=pltpu.SMEM), vmem],
        out_specs=vmem,
        out_shape=jax.ShapeDtypeStruct((count // cores, height, width), jnp.bfloat16),
        compiler_params=params(8),
        name="pair_sum",
    )(core, pieces)


def second_kernel(
    pre_ref, adj_ref, two_ref, three_ref, cot_ref, logits_ref, grad_ref
):
    count, height, width = pre_ref.shape
    halves = adj_ref.shape[0] // height
    strips = [
        jnp.concatenate([pre_ref[t * halves + h] for h in range(halves)], axis=0)
        for t in range(count // halves)
    ]
    pre = jnp.concatenate(strips, axis=1).astype(jnp.float32)
    gate = jax.nn.sigmoid(pre)
    first_hidden = (pre * gate).astype(jnp.bfloat16)
    slope = (gate + pre * gate * (1.0 - gate)).astype(jnp.bfloat16).astype(jnp.float32)
    adjacency = adj_ref[...]
    inv = 1.0 / jnp.sum(adjacency.astype(jnp.float32), axis=1, keepdims=True)
    mixed = (dot(adjacency, first_hidden) * inv).astype(jnp.bfloat16)
    pre_two = dot(mixed, two_ref[...])
    gate_two = jax.nn.sigmoid(pre_two)
    second_hidden = (pre_two * gate_two).astype(jnp.bfloat16)
    across = ((1,), (1,))
    logits_ref[...] = dot(three_ref[...], second_hidden, across).astype(jnp.bfloat16)
    slope_two = gate_two + pre_two * gate_two * (1.0 - gate_two)
    back_two = dot(cot_ref[...], three_ref[...], ((0,), (0,)))
    grad_two = (back_two * slope_two).astype(jnp.bfloat16)
    grad_mixed = dot(grad_two, two_ref[...], across) * inv
    high = grad_mixed.astype(jnp.bfloat16)
    rest = grad_mixed - high.astype(jnp.float32)
    middle = rest.astype(jnp.bfloat16)
    low = (rest - middle.astype(jnp.float32)).astype(jnp.bfloat16)
    down = ((0,), (0,))
    grad_hidden = dot(adjacency, high, down) + (
        dot(adjacency, middle, down) + dot(adjacency, low, down)
    )
    grad_one = (grad_hidden * slope).astype(jnp.bfloat16)
    quarter = grad_ref.shape[2]
    for x in range(grad_ref.shape[0]):
        grad_ref[x] = grad_one[:, x * quarter : (x + 1) * quarter]


def second_layer(pre, adjacency, weight_two, weight_three, cotangent):
    rows = adjacency.shape[0]
    hidden = weight_two.shape[0]
    classes = weight_three.shape[0]
    vmem = pl.BlockSpec(memory_space=pltpu.VMEM)
    return pl.pallas_call(
        second_kernel,
        in_specs=[vmem] * 5,
        out_specs=[vmem] * 2,
        out_shape=[
            jax.ShapeDtypeStruct((classes, rows), jnp.bfloat16),
            jax.ShapeDtypeStruct((XS, rows, hidden // XS), jnp.bfloat16),
        ],
        compiler_params=params(24),
        name="second_layer",
    )(pre, adjacency, weight_two, weight_three, cotangent)


def gradient_kernel(place_ref, *refs):
    operands, grad_ref, out_ref = refs[:-2], refs[-2], refs[-1]
    width = operands[0].shape[1]
    for half in range(2):
        total = None
        for shift in range(XS):
            source = lax.rem(place_ref[0] + (XS - shift), XS)
            rows = operands[half * XS + shift][...]
            part = dot(rows, grad_ref[source], ((0,), (0,)))
            total = part if total is None else total + part
        out_ref[half * width : (half + 1) * width, :] = total.astype(jnp.bfloat16)


def gradient_part(place, own, mean, grad):
    vmem = pl.BlockSpec(memory_space=pltpu.VMEM)
    return pl.pallas_call(
        gradient_kernel,
        in_specs=[pl.BlockSpec(memory_space=pltpu.SMEM)] + [vmem] * (2 * XS + 1),
        out_specs=vmem,
        out_shape=jax.ShapeDtypeStruct((2 * own[0].shape[1], grad.shape[2]), jnp.bfloat16),
        compiler_params=params(16),
        name="gradient_part",
    )(place, *own, *mean, grad)


def spread_kernel(recv_ref, out_ref):
    sums = recv_ref[0].astype(jnp.float32)
    for i in range(1, recv_ref.shape[0]):
        sums = sums + recv_ref[i].astype(jnp.float32)
    piece = sums.astype(jnp.bfloat16)
    for i in range(out_ref.shape[0]):
        out_ref[i] = piece


def spread(recv, copies):
    vmem = pl.BlockSpec(memory_space=pltpu.VMEM)
    return pl.pallas_call(
        spread_kernel,
        in_specs=[vmem],
        out_specs=vmem,
        out_shape=jax.ShapeDtypeStruct((copies,) + recv.shape[1:], recv.dtype),
        compiler_params=params(8),
        name="sum_and_spread",
    )(recv)


def assemble_kernel(recv_hbm, self_hbm, neigh_hbm, sem):
    height, hidden = self_hbm.shape
    width = recv_hbm.shape[1]
    copies = []
    for x in range(hidden // width):
        for i, out in enumerate((self_hbm, neigh_hbm)):
            source = recv_hbm.at[pl.ds((2 * x + i) * height, height), :]
            copies.append(
                pltpu.make_async_copy(source, out.at[:, pl.ds(x * width, width)], sem.at[2 * x + i])
            )
    for copy in copies:
        copy.start()
    for copy in copies:
        copy.wait()


def assemble(recv):
    total, width = recv.shape
    height = total // XS // 2
    shape = jax.ShapeDtypeStruct((height, XS * width), recv.dtype)
    return pl.pallas_call(
        assemble_kernel,
        in_specs=[pl.BlockSpec(memory_space=pl.ANY)],
        out_specs=[pl.BlockSpec(memory_space=pltpu.HBM)] * 2,
        out_shape=[shape] * 2,
        scratch_shapes=[pltpu.SemaphoreType.DMA((2 * XS,))],
        compiler_params=params(8),
        name="assemble",
    )(recv)


def exchange(pieces, axis):
    return lax.all_to_all(pieces, axis, split_axis=0, concat_axis=0, tiled=True)


def shift_x(array, steps):
    return lax.ppermute(array, "x", [(i, (i + steps) % XS) for i in range(XS)])


def body(
    features,
    own_features,
    neigh_index,
    neigh_count,
    degree,
    local_index,
    local_count,
    self_weight,
    neigh_weight,
    weight_two,
    weight_three,
    cotangent,
):
    groups = lax.axis_size(NODE)
    splits = lax.axis_size(FEAT)
    own_rows, width = own_features.shape
    slots = neigh_index.shape[2]
    per_x = own_rows * (groups // XS)

    place = lax.axis_index("x").reshape(1).astype(jnp.int32)
    payloads = make_payloads(place, neigh_index[0].T, neigh_count, features)
    arrived = [shift_x(payloads[s], s) for s in (2, 1, 3)]
    running = gather_sum(slots, per_x, jnp.float32, None, payloads[:1])
    running = gather_sum(slots, per_x, jnp.float32, running, arrived[1:])
    parts = gather_sum(slots, per_x, jnp.bfloat16, running, arrived[:1], staged=True)
    own = [shift_x(own_features, s) for s in range(1, XS)]
    recv = exchange(parts.reshape(groups // XS, own_rows, width), "z")
    recv, *own = lax.optimization_barrier((recv, *own))
    mean_rows, pieces = first_layer(
        recv,
        degree[:, None].astype(jnp.float32),
        own_features,
        self_weight,
        neigh_weight,
        splits,
    )
    mean = [shift_x(mean_rows, s) for s in range(1, XS)]
    core = lax.axis_index("c").reshape(1).astype(jnp.int32)
    paired = pair_sum(core, lax.all_gather(pieces, "c", axis=0, tiled=False))
    paired, mean[0] = lax.optimization_barrier((exchange(paired, "y"), mean[0]))
    pre_copies = spread(paired, paired.shape[0])
    pre = lax.all_gather(exchange(pre_copies, "y"), "c", axis=0, tiled=True)
    pre, mean[1], mean[2] = lax.optimization_barrier((pre, mean[1], mean[2]))

    slot_ids = jnp.arange(local_index.shape[1], dtype=jnp.int32)
    live_slots = slot_ids[None, :] < local_count[:, None]
    slot_hits = (
        local_index[:, :, None] == jnp.arange(own_rows, dtype=jnp.int32)[None, None, :]
    ) & live_slots[:, :, None]
    adjacency = (
        jnp.sum(slot_hits.astype(jnp.float32), axis=1) + jnp.eye(own_rows, dtype=jnp.float32)
    ).astype(jnp.bfloat16)
    logits, grad_one = second_layer(
        pre, adjacency, weight_two, weight_three.T, cotangent.T
    )
    grad_part = gradient_part(place, [own_features] + own, [mean_rows] + mean, exchange(grad_one, "x"))
    quarter = grad_part.shape[1]
    grad_recv = exchange(grad_part.reshape(groups // XS, -1, quarter), "z")
    part = exchange(spread(grad_recv, groups // XS), "z")
    grads = exchange(spread(part.reshape(1, -1, quarter), XS), "x")
    grad_self, grad_neigh = assemble(grads.reshape(-1, quarter))
    return (grad_self, grad_neigh, logits.T)


def solution(mesh):
    nodes, feats = mesh.devices.shape
    fine = Mesh(mesh.devices.reshape(XS, nodes // XS, feats // 2, 2), ("x", "z", "y", "c"))
    in_specs = (
        P(NODE, FEAT),
        P(NODE, FEAT),
        P(NODE, None, None),
        P(NODE, None),
        P(NODE),
        P(NODE, None),
        P(NODE),
        P(FEAT, None),
        P(FEAT, None),
        P(),
        P(),
        P(NODE, None),
    )
    out_specs = (P(FEAT, None), P(FEAT, None), P(NODE, None))
    return jax.shard_map(body, mesh=fine, in_specs=in_specs, out_specs=out_specs, check_vma=False)
```
